256 devices in a mesh: line: 16 (over z, x_hi), seg: 16 (over y, x_lo, core).
Axes of the slice: x: 4 (x_hi: 2, x_lo: 2; x = x_hi * 2 + x_lo), y: 4, z: 8, core: 2. Of those that a mesh axis runs over, the one named last changes fastest.
Arguments:
- feats: float32 [16, 32768, 512], P('line', 'seg'), as said below
- norm_gain: float32 [512], replicated, may hold values from 0.1 to 1.9
- w_qkv: float32 [512, 1536], replicated, as said below
- w_out: float32 [512, 512], replicated, may hold values from -0.25 to 0.25
- counts: int32 [16, 256], P('line', 'seg'), may hold values from 1 to 128
- partner: int32 [16, 16], P('line', 'seg'), may hold values from 0 to 1, as said below
- cross_list: int32 [16, 256, 2], P('line', 'seg'), may hold values from -1 to 15, as said below
Outputs:
- mixed: float32 [16, 32768, 512], P('line', 'seg')
The draws below stay inside these ranges and needn't reach their ends.
Inputs may be any that keep to these rules, and one draw needn't show every extreme that they name: partner of the first line is 1 and of the last line is 0. `cross_list`: the entries of a row that are not -1 are distinct. `w_qkv`: entries have magnitude under 4. `feats`: entries have magnitude under 60.
All inputs are finite; a program needn't handle non-finite values.
Results may differ from the reference program's by a relative error of at most 0.0003.
Values sent between devices are 32-bit elements; how exact they have to be, the bound alone decides.
A program may use at most 192 MiB of HBM per device.

```python
import math
import jax
import jax.numpy as jnp
from jax import lax

C = 512
HEADS = 8
BLK = 128
LIST = 2
QB = 16
LINES = 16
SEGS = 16
NBLK = 256
PTS = 32768


def draw_feats(key, part):
    key = jax.random.fold_in(key, 11)
    first_key = jax.random.fold_in(key, 0)
    base = jax.random.normal(first_key, (LINES, PTS, C), jnp.float32)
    base = jnp.clip(base, -6.0, 6.0)
    return base


def draw_w_qkv(key, part):
    key = jax.random.fold_in(key, 23)
    first_key, second_key = jax.random.split(key, 2)
    query_part = jax.random.normal(first_key, (C, C), jnp.float32) / math.sqrt(C)
    rest = jax.random.normal(second_key, (C, 2 * C), jnp.float32) / math.sqrt(C)
    return jnp.clip(jnp.concatenate([query_part, rest], axis=1), -3.9, 3.9)


def draw_partner(key, part):
    key = jax.random.fold_in(key, 37)
    toward = jax.random.randint(key, (LINES, SEGS), 0, 2)
    line_ids = jnp.arange(LINES, dtype=jnp.int32)[:, None]
    toward = jnp.where(line_ids == 0, 1, toward)
    toward = jnp.where(line_ids == LINES - 1, 0, toward)
    return toward.astype(jnp.int32)


def draw_cross_list(key, part):
    key = jax.random.fold_in(key, 41)
    first_key, second_key = jax.random.split(key)
    ranks = jax.random.randint(first_key, (LINES, NBLK, QB), 0, 1 << 20) * QB + jnp.arange(QB, dtype=jnp.int32)
    ordered = jnp.argsort(ranks, axis=-1)[..., :LIST].astype(jnp.int32)
    dropped = jax.random.randint(second_key, (LINES, NBLK, LIST), 0, 4) == 0
    return jnp.where(dropped, -1, ordered).astype(jnp.int32)


def place_ends(values, rng, low, largest):
    longest = values.shape.index(max(values.shape))
    spots = []
    for shift in (0, 1):
        where = [jax.random.randint(jax.random.fold_in(rng, axis), (), 0, length) for axis, length in enumerate(values.shape)]
        where[longest] = (where[longest] + shift) % values.shape[longest]
        spots.append(tuple(where))
    return values.at[spots[0]].set(low).at[spots[1]].set(largest)


def centred(own_key, shape, scale, bound, kind=jnp.bfloat16):
    values = scale * jax.random.normal(own_key, shape, jnp.float32)
    return jnp.clip(values, min=-bound, max=bound).astype(kind)


def setup_inputs(seed: int = 0) -> dict:
    arg_keys = jax.random.split(jax.random.key(seed), 8)
    feats = draw_feats(jax.random.fold_in(arg_keys[7], 71), 0)
    norm_gain = jnp.clip(1.0 + 0.18 * jax.random.normal(arg_keys[1], (C,), jnp.float32), 0.1, 1.9)
    w_qkv = draw_w_qkv(jax.random.fold_in(arg_keys[7], 71), 0)
    w_out = centred(arg_keys[3], (C, C), C ** -0.5, 0.25, jnp.float32)
    counts = place_ends(jax.random.randint(arg_keys[4], (LINES, NBLK), 1, 129), jax.random.fold_in(arg_keys[4], 1), 1, 128).astype(jnp.int32)
    partner = draw_partner(jax.random.fold_in(arg_keys[7], 71), 0)
    cross_list = draw_cross_list(jax.random.fold_in(arg_keys[7], 71), 0)
    return dict(feats=feats, norm_gain=norm_gain, w_qkv=w_qkv, w_out=w_out, counts=counts, partner=partner, cross_list=cross_list)


def layer_norm(values, gain):
    center = values - lax.optimization_barrier(jnp.mean(values, axis=-1, keepdims=True))
    spread = lax.optimization_barrier(jnp.mean(center * center, axis=-1, keepdims=True))
    return center * lax.rsqrt(spread + 1e-05) * gain

def attend_blocks(queries, key_vals, key_mask, width):
    head_size = width // HEADS
    groups = queries.shape[0]
    q_heads = queries.reshape(groups, BLK, HEADS, head_size)
    k_heads = key_vals[..., :width].reshape(groups, -1, HEADS, head_size)
    v_heads = key_vals[..., width:].reshape(groups, -1, HEADS, head_size)
    scores = jnp.einsum('bqhd,bkhd->bhqk', q_heads, k_heads, precision=lax.Precision.HIGHEST) * head_size ** (-0.5)
    scores = jnp.where(key_mask[:, None, None, :], scores, -1e+30)
    top = lax.optimization_barrier(jnp.max(scores, axis=-1, keepdims=True))
    weights = jnp.where(key_mask[:, None, None, :], jnp.exp(scores - top), 0.0)
    total = lax.optimization_barrier(jnp.sum(weights, axis=-1))
    summed = jnp.einsum('bhqk,bkhd->bqhd', weights, v_heads, precision=lax.Precision.HIGHEST)
    summed = summed / jnp.transpose(total, (0, 2, 1))[..., None]
    return summed.reshape(groups * BLK, width)

def reference(feats, norm_gain, w_qkv, w_out, counts, partner, cross_list):
    lines = feats.shape[0]
    width = feats.shape[2]
    nblocks = counts.shape[1]
    normed = layer_norm(feats, norm_gain)
    qkv = jnp.einsum('lpc,cd->lpd', normed, w_qkv, precision=lax.Precision.HIGHEST)
    queries = qkv[..., :width]
    key_vals = qkv[..., width:].reshape(lines, nblocks, BLK, 2 * width)
    offsets = jnp.arange(BLK, dtype=jnp.int32)
    live = offsets[None, None, :] < counts[:, :, None]
    padded_kv = jnp.pad(key_vals, ((0, 0), (1, 1), (0, 0), (0, 0)))
    padded_live = jnp.pad(live, ((0, 0), (1, 1), (0, 0)))
    seg_of = (jnp.arange(nblocks, dtype=jnp.int32) // QB).astype(jnp.int32)

    def one_line(line_index):
        own_kv = padded_kv[line_index]
        own_live = padded_live[line_index]
        local_kv = jnp.stack([own_kv[0:nblocks], own_kv[1:nblocks + 1], own_kv[2:nblocks + 2]], axis=1)
        local_live = jnp.stack([own_live[0:nblocks], own_live[1:nblocks + 1], own_live[2:nblocks + 2]], axis=1)
        toward = partner[line_index][seg_of]
        other = jnp.clip(line_index + 2 * toward - 1, 0, lines - 1).astype(jnp.int32)
        listed = cross_list[line_index]
        picked = (seg_of[:, None] * QB + jnp.maximum(listed, 0)).astype(jnp.int32)
        cross_kv = key_vals[other[:, None], picked]
        cross_live = live[other[:, None], picked] & (listed >= 0)[:, :, None]
        all_kv = jnp.concatenate([local_kv, cross_kv], axis=1).reshape(nblocks, -1, 2 * width)
        all_live = jnp.concatenate([local_live, cross_live], axis=1).reshape(nblocks, -1)
        own_q = queries[line_index].reshape(nblocks, BLK, width)
        attended = attend_blocks(own_q, all_kv, all_live, width)
        result = feats[line_index] + jnp.dot(attended, w_out, precision=lax.Precision.HIGHEST)
        return jnp.where(live[line_index].reshape(-1)[:, None], result, 0.0)
    return lax.map(one_line, jnp.arange(lines, dtype=jnp.int32))
```

```python
import functools
import math

import jax
import jax.numpy as jnp
from jax import lax
from jax.experimental import pallas as pl
from jax.experimental.pallas import tpu as pltpu
from jax.sharding import PartitionSpec as P

MESH = pl.DeviceIdType.MESH
F32, BF16 = jnp.float32, jnp.bfloat16
HEADS = 8
BLK = 128
DIM = 64
PAIR = 2 * DIM
RING = 8
MASKED = -1e30
NT = (((1,), (1,)), ((), ()))


def split(x):
    high = x.astype(BF16)
    return high, (x - high.astype(F32)).astype(BF16)


def dot(a, b):
    return jnp.dot(a, b, preferred_element_type=F32)


def dot3(ah, al, bh, bl):
    return dot(ah, bh) + dot(al, bh) + dot(ah, bl)


def normalize(x):
    center = x - jnp.mean(x, axis=-1, keepdims=True)
    spread = jnp.mean(center * center, axis=-1, keepdims=True)
    return center * lax.rsqrt(spread + 1e-05)


def iota(shape, dim):
    return lax.broadcasted_iota(jnp.int32, shape, dim)


def swap(x):
    return pltpu.roll(x, DIM, 1)


def kernel(
    blocks,
    feats, gain, w_qkv, w_out, counts, counts_row, partner, listed,
    out,
    own, near, far, halo, cnt,
    w_hi, w_lo, q_all, k_ring, v_ring, k_strip, v_strip, mixed, lse_all,
    x_send, x_recv, z_send, z_recv, h_send, h_recv, c_send, c_recv,
    own_sem, w_sem, out_sem,
):
    groups = blocks // 2
    rows = 2 * BLK
    width = own.shape[1]
    pairs = width // PAIR
    line, seg = lax.axis_index("line"), lax.axis_index("seg")
    lines, segs = lax.axis_size("line"), lax.axis_size("seg")
    odd = lax.rem(line, 2)
    mate = line + 1 - 2 * odd
    ahead = lax.rem(line + 2 - 4 * odd + lines, lines)
    behind = lax.rem(line - 2 + 4 * odd + lines, lines)
    right, left = lax.rem(seg + 1, segs), lax.rem(seg + segs - 1, segs)

    def group_rows(i):
        return pl.ds(pl.multiple_of(i * rows, rows), rows)

    def block_rows(b):
        return pl.ds(pl.multiple_of(b * BLK, BLK), BLK)

    def own_copy(i):
        return pltpu.make_async_copy(feats.at[group_rows(i)], own.at[group_rows(i)], own_sem.at[i])

    def w_copy(j):
        source = w_out if j == 3 else w_qkv.at[:, pl.ds(j * width, width)]
        return pltpu.make_async_copy(source, mixed.at[pl.ds(j * width, width)], w_sem.at[j])

    def out_copy(i):
        return pltpu.make_async_copy(mixed.at[group_rows(i)], out.at[group_rows(i)], out_sem.at[i])

    def remote(source, target, send, recv, device):
        return pltpu.make_async_remote_copy(
            src_ref=source, dst_ref=target, send_sem=send, recv_sem=recv,
            device_id=device, device_id_type=MESH,
        )

    def x_copy(c):
        return remote(feats.at[block_rows(c)], near.at[block_rows(c)], x_send.at[c], x_recv.at[c], (mate, seg))

    def z_copy(c):
        return remote(near.at[block_rows(c)], far.at[block_rows(c)], z_send.at[c], z_recv.at[c], (ahead, seg))

    def h_copy(j):
        b, device = ((blocks - 1), (line, right)) if j == 0 else (0, (line, left))
        return remote(feats.at[pl.ds(b * BLK, BLK)], halo.at[pl.ds(j * BLK, BLK)], h_send.at[j], h_recv.at[j], device)

    def c_copy(j):
        source = cnt.at[2] if j == 3 else counts_row
        device = ((line, right), (line, left), (mate, seg), (ahead, seg))[j]
        return remote(source, cnt.at[j], c_send.at[j], c_recv.at[j], device)

    barrier = pltpu.get_barrier_semaphore()
    for device in ((mate, seg), (ahead, seg), (behind, seg), (line, right), (line, left)):
        pl.semaphore_signal(barrier, inc=1, device_id=device, device_id_type=MESH)
    for j in range(4):
        w_copy(j).start()
    for i in range(groups):
        own_copy(i).start()
    pl.semaphore_wait(barrier, 5)
    for j in range(3):
        c_copy(j).start()
    for j in range(2):
        h_copy(j).start()

    @pl.loop(0, blocks)
    def _(c):
        x_copy(c).start()

    for j in range(4):
        w_copy(j).wait()
        w = mixed[j * width : (j + 1) * width]
        if j < 3:
            w = w * gain[...]
        if j == 0:
            w = w * (DIM**-0.5 * math.log2(math.e))
        w_hi[:, j * width : (j + 1) * width], w_lo[:, j * width : (j + 1) * width] = split(w)

    def low(n):
        return iota((n, PAIR), 1) < DIM

    def mark(n):
        return iota((n, PAIR), 1) == DIM

    def weights(j, p):
        columns = pl.ds(j * width + p * 2 * PAIR, 2 * PAIR)
        return w_hi[:, columns], w_lo[:, columns]

    def bias_of(count):
        dead = (iota((BLK, PAIR), 0) >= count) & mark(BLK)
        return jnp.where(dead, MASKED, 0.0)

    def count_in(row, b):
        return jnp.sum(jnp.where(iota(row.shape, 1) == b, row, 0.0), axis=1, keepdims=True).astype(jnp.int32)

    def store_keys(xh, xl, k_ref, v_ref, slots, bias):
        lo = low(rows)
        for p in range(pairs // 2):
            both = dot3(xh, xl, *weights(1, p))
            for half in range(2):
                h = 4 * p + 2 * half
                k = both[:, half * PAIR : (half + 1) * PAIR]
                kh = k.astype(BF16).astype(F32)
                kl = k - kh
                kh_, kl_ = swap(kh), swap(kl)
                for head, a, b in ((h, jnp.where(lo, kh, kl_), kh), (h + 1, jnp.where(lo, kh_, kl), kh_)):
                    a = a.astype(BF16)
                    b = jnp.where(lo, b, bias).astype(BF16)
                    for n, slot in enumerate(slots):
                        k_ref[slot, head, :, :PAIR] = a[n * BLK : (n + 1) * BLK]
                        k_ref[slot, head, :, PAIR:] = b[n * BLK : (n + 1) * BLK]
        for p in range(pairs // 2):
            both = dot3(xh, xl, *weights(2, p))
            for half in range(2):
                h = 4 * p + 2 * half
                v = both[:, half * PAIR : (half + 1) * PAIR]
                vh = v.astype(BF16).astype(F32)
                vl = v - vh
                for head, a in ((h, jnp.where(lo, vh, swap(vl))), (h + 1, jnp.where(lo, swap(vh), vl))):
                    a = a.astype(BF16)
                    for n, slot in enumerate(slots):
                        v_ref[slot, head] = a[n * BLK : (n + 1) * BLK]

    def own_group(i):
        own_copy(i).wait()
        xh, xl = split(normalize(own[group_rows(i)]))
        for p in range(pairs // 2):
            q_all[group_rows(i), p * 2 * PAIR : (p + 1) * 2 * PAIR] = dot3(xh, xl, *weights(0, p))
        bias = jnp.concatenate([bias_of(counts[0, 2 * i]), bias_of(counts[0, 2 * i + 1])], axis=0)
        slot = lax.rem(2 * i, RING)
        store_keys(xh, xl, k_ring, v_ring, (slot, slot + 1), bias)

    def halo_group():
        for j in range(2):
            h_copy(j).wait()
            c_copy(j).wait()
        xh, xl = split(normalize(halo[...]))
        before = jnp.where(seg == 0, 0, count_in(cnt[0, 0:1], blocks - 1))
        after = jnp.where(seg == segs - 1, 0, count_in(cnt[1, 0:1], 0))
        bias = jnp.concatenate([bias_of(before), bias_of(after)], axis=0)
        store_keys(xh, xl, k_ring, v_ring, (RING - 1, RING), bias)

    use_near = lax.rem(partner[0, 0] + odd, 2) == 1

    def strip_group(i):
        z_copy(2 * i).wait_recv()
        z_copy(2 * i + 1).wait_recv()
        x = jnp.where(use_near, near[group_rows(i)], far[group_rows(i)])
        row = jnp.where(use_near, cnt[2, 0:1], cnt[3, 0:1])
        xh, xl = split(normalize(x))
        bias = jnp.concatenate([bias_of(count_in(row, 2 * i)), bias_of(count_in(row, 2 * i + 1))], axis=0)
        store_keys(xh, xl, k_strip, v_strip, (2 * i, 2 * i + 1), bias)

    def queries(r, p):
        q = q_all[r, p * PAIR : (p + 1) * PAIR]
        lo = low(BLK)
        one = jnp.where(mark(BLK), 1.0, 0.0)
        qh = q.astype(BF16).astype(F32)
        ql = q - qh
        qh_, ql_ = swap(qh), swap(ql)
        first = jnp.concatenate([jnp.where(lo, qh, qh_), jnp.where(lo, ql, one)], axis=1).astype(BF16)
        second = jnp.concatenate([jnp.where(lo, qh_, qh), jnp.where(lo, ql_, one)], axis=1).astype(BF16)
        return first, second

    def weigh(s, top, v):
        e = jnp.exp2(s - top)
        eh, el = split(e)
        summed = dot(jnp.concatenate([eh, el], axis=0), v)
        summed = summed[:BLK] + summed[BLK:]
        return summed + swap(summed), jnp.sum(e, axis=1, keepdims=True)

    def local_block(b, slots):
        r = block_rows(b)
        lo = low(BLK)
        for p in range(pairs):
            results = []
            for n, q in enumerate(queries(r, p)):
                h = 2 * p + n
                k = jnp.concatenate([k_ring[slot, h] for slot in slots], axis=0)
                v = jnp.concatenate([v_ring[slot, h] for slot in slots], axis=0)
                s = lax.dot_general(q, k, NT, preferred_element_type=F32)
                top = jnp.max(s, axis=1, keepdims=True)
                summed, total = weigh(s, top, v)
                results.append((summed / total, jnp.broadcast_to(top + jnp.log2(total), (BLK, PAIR))))
            columns = slice(p * PAIR, (p + 1) * PAIR)
            mixed[r, columns] = jnp.where(lo, results[0][0], results[1][0])
            lse_all[r, columns] = jnp.where(lo, results[0][1], results[1][1])

    def local_group(i, last=False):
        for n in range(2):
            b = 2 * i + n
            slots = [lax.rem(b - 1 + j + RING, RING) for j in range(3)]
            if last and n == 1:
                slots[2] = RING
            local_block(b, slots)

    for h in range(HEADS):
        k_strip[blocks, h, :, :PAIR] = jnp.zeros((BLK, PAIR), BF16)
        k_strip[blocks, h, :, PAIR:] = bias_of(0).astype(BF16)
        v_strip[blocks, h] = jnp.zeros((BLK, PAIR), BF16)

    @pl.loop(0, groups)
    def _(i):
        x_copy(2 * i).wait_recv()
        z_copy(2 * i).start()

        @pl.when(i == 0)
        def _():
            c_copy(2).wait()
            c_copy(3).start()

        own_group(i)
        x_copy(2 * i + 1).wait_recv()
        z_copy(2 * i + 1).start()

        @pl.when(i == 0)
        def _():
            halo_group()
            c_copy(3).wait()

        @pl.when(i > 0)
        def _():
            local_group(i - 1)
            strip_group(i - 1)

    local_group(groups - 1, last=True)
    strip_group(groups - 1)

    @pl.loop(0, groups)
    def _(i):
        lo = low(BLK)
        attended = []
        for n in range(2):
            b = 2 * i + n
            r = block_rows(b)
            picks = [jnp.where(listed[b, j] < 0, blocks, listed[b, j]) for j in range(2)]
            tiles = []
            for p in range(pairs):
                columns = slice(p * PAIR, (p + 1) * PAIR)
                before = mixed[r, columns]
                lse_pair = lse_all[r, columns]
                results = []
                for m, q in enumerate(queries(r, p)):
                    h = 2 * p + m
                    k = jnp.concatenate([k_strip[pick, h] for pick in picks], axis=0)
                    v = jnp.concatenate([v_strip[pick, h] for pick in picks], axis=0)
                    s = lax.dot_general(q, k, NT, preferred_element_type=F32)
                    lse = lse_pair[:, m * DIM : m * DIM + 1]
                    top = jnp.maximum(jnp.max(s, axis=1, keepdims=True), lse)
                    summed, total = weigh(s, top, v)
                    weight = jnp.exp2(lse - top)
                    results.append((before * weight + summed) / (total + weight))
                tiles.append(jnp.where(lo, results[0], results[1]))
            attended.append(jnp.concatenate(tiles, axis=1))
        ah, al = split(jnp.concatenate(attended, axis=0))
        r = group_rows(i)
        row = iota((BLK, 2 * PAIR), 0)
        live = jnp.concatenate([row < counts[0, 2 * i + n] for n in range(2)], axis=0)
        for p in range(pairs // 2):
            columns = slice(p * 2 * PAIR, (p + 1) * 2 * PAIR)
            result = own[r, columns] + dot3(ah, al, *weights(3, p))
            mixed[r, columns] = jnp.where(live, result, 0.0)
        out_copy(i).start()

    @pl.loop(0, blocks)
    def _(c):
        x_copy(c).wait_send()
        z_copy(c).wait_send()

    for i in range(groups):
        out_copy(i).wait()


def body(feats, norm_gain, w_qkv, w_out, counts, partner, cross_list):
    points = feats[0]
    rows, width = points.shape
    blocks = counts.shape[1]
    groups = blocks // 2
    counts_row = jnp.zeros((8, BLK), F32).at[0, :blocks].set(counts[0].astype(F32))
    hbm = pl.BlockSpec(memory_space=pl.ANY)
    vmem = pl.BlockSpec(memory_space=pltpu.VMEM)
    smem = pl.BlockSpec(memory_space=pltpu.SMEM)
    dma = pltpu.SemaphoreType.DMA
    mixed = pl.pallas_call(
        functools.partial(kernel, blocks),
        out_shape=jax.ShapeDtypeStruct((rows, width), F32),
        in_specs=[hbm, vmem, hbm, hbm, smem, vmem, smem, smem],
        out_specs=hbm,
        scratch_shapes=[
            pltpu.VMEM((rows, width), F32),
            pltpu.VMEM((rows, width), F32),
            pltpu.VMEM((rows, width), F32),
            pltpu.VMEM((2 * BLK, width), F32),
            pltpu.VMEM((4, 8, BLK), F32),
            pltpu.VMEM((width, 4 * width), BF16),
            pltpu.VMEM((width, 4 * width), BF16),
            pltpu.VMEM((rows, width), F32),
            pltpu.VMEM((RING + 1, HEADS, BLK, 2 * PAIR), BF16),
            pltpu.VMEM((RING + 1, HEADS, BLK, PAIR), BF16),
            pltpu.VMEM((blocks + 1, HEADS, BLK, 2 * PAIR), BF16),
            pltpu.VMEM((blocks + 1, HEADS, BLK, PAIR), BF16),
            pltpu.VMEM((rows, width), F32),
            pltpu.VMEM((rows, width), F32),
            dma((blocks,)), dma((blocks,)), dma((blocks,)), dma((blocks,)),
            dma((2,)), dma((2,)), dma((4,)), dma((4,)),
            dma((groups,)), dma((4,)), dma((groups,)),
        ],
        compiler_params=pltpu.CompilerParams(
            collective_id=0, has_side_effects=True, vmem_limit_bytes=60 * 1024 * 1024
        ),
    )(points, norm_gain.reshape(width, 1), w_qkv, w_out, counts, counts_row, partner, cross_list[0])
    return mixed[None]


def solution(mesh):
    in_specs = (
        P("line", "seg", None),
        P(),
        P(),
        P(),
        P("line", "seg"),
        P("line", "seg"),
        P("line", "seg", None),
    )
    out_specs = P("line", "seg", None)
    return jax.shard_map(body, mesh=mesh, in_specs=in_specs, out_specs=out_specs, check_vma=False)
```

```python
import functools
import math

import jax
import jax.numpy as jnp
from jax import lax
from jax.experimental import pallas as pl
from jax.experimental.pallas import tpu as pltpu
from jax.sharding import PartitionSpec as P

MESH = pl.DeviceIdType.MESH
F32, BF16 = jnp.float32, jnp.bfloat16
HEADS = 8
BLK = 128
DIM = 64
PAIR = 2 * DIM
RING = 8
MASKED = -1e30
NT = (((1,), (1,)), ((), ()))


def split(x):
    high = x.astype(BF16)
    return high, (x - high.astype(F32)).astype(BF16)


def dot(a, b):
    return jnp.dot(a, b, preferred_element_type=F32)


def dot3(ah, al, bh, bl):
    return dot(ah, bh) + dot(al, bh) + dot(ah, bl)


def normalize(x, gain):
    center = x - jnp.mean(x, axis=-1, keepdims=True)
    spread = jnp.mean(center * center, axis=-1, keepdims=True)
    return center * lax.rsqrt(spread + 1e-05) * gain


def iota(shape, dim):
    return lax.broadcasted_iota(jnp.int32, shape, dim)


def dot_nt(a, b):
    return lax.dot_general(a, b, NT, preferred_element_type=F32)


def swap(x):
    return pltpu.roll(x, DIM, 1)


def kernel(
    blocks,
    feats, gain, w_qkv, w_out, counts, partner, listed,
    out,
    own, near, far, halo, counts_row, cnt,
    w_hi, w_lo, q_hi, q_lo, k_ring, v_ring, k_strip, v_strip, summed, tops, totals,
    x_send, x_recv, z_send, z_recv, h_send, h_recv, c_send, c_recv,
    own_sem, w_sem, out_sem,
):
    groups = blocks // 2
    rows = 2 * BLK
    width = own.shape[1]
    pairs = width // PAIR
    line, seg = lax.axis_index("line"), lax.axis_index("seg")
    lines, segs = lax.axis_size("line"), lax.axis_size("seg")
    odd = lax.rem(line, 2)
    mate = line + 1 - 2 * odd
    ahead = lax.rem(line + 2 - 4 * odd + lines, lines)
    behind = lax.rem(line - 2 + 4 * odd + lines, lines)
    right, left = lax.rem(seg + 1, segs), lax.rem(seg + segs - 1, segs)

    def group_rows(i):
        return pl.ds(pl.multiple_of(i * rows, rows), rows)

    def block_rows(b):
        return pl.ds(pl.multiple_of(b * BLK, BLK), BLK)

    def own_copy(i):
        return pltpu.make_async_copy(feats.at[group_rows(i)], own.at[group_rows(i)], own_sem.at[i])

    def w_copy(j):
        source = w_qkv.at[:, pl.ds(j * rows, rows)] if j < 6 else w_out.at[:, pl.ds((j - 6) * rows, rows)]
        return pltpu.make_async_copy(source, summed.at[j], w_sem.at[j])

    def out_copy(i):
        return pltpu.make_async_copy(own.at[group_rows(i)], out.at[group_rows(i)], out_sem.at[i])

    def remote(source, target, send, recv, device):
        return pltpu.make_async_remote_copy(
            src_ref=source, dst_ref=target, send_sem=send, recv_sem=recv,
            device_id=device, device_id_type=MESH,
        )

    def x_copy(c):
        return remote(feats.at[block_rows(c)], near.at[block_rows(c)], x_send.at[c], x_recv.at[c], (mate, seg))

    def z_copy(c):
        return remote(near.at[block_rows(c)], far.at[block_rows(c)], z_send.at[c], z_recv.at[c], (ahead, seg))

    def h_copy(j):
        b, device = ((blocks - 1), (line, right)) if j == 0 else (0, (line, left))
        return remote(feats.at[pl.ds(b * BLK, BLK)], halo.at[pl.ds(j * BLK, BLK)], h_send.at[j], h_recv.at[j], device)

    def c_copy(j):
        source = cnt.at[2] if j == 3 else counts_row
        device = ((line, right), (line, left), (mate, seg), (ahead, seg))[j]
        return remote(source, cnt.at[j], c_send.at[j], c_recv.at[j], device)

    barrier = pltpu.get_barrier_semaphore()
    for device in ((mate, seg), (ahead, seg), (behind, seg), (line, right), (line, left)):
        pl.semaphore_signal(barrier, inc=1, device_id=device, device_id_type=MESH)
    for i in range(groups):
        own_copy(i).start()
    for j in range(8):
        w_copy(j).start()
    lane = iota((8, BLK), 1)
    filled = jnp.zeros((8, BLK), F32)
    for b in range(blocks):
        filled = jnp.where(lane == b, counts[0, b].astype(F32), filled)
    counts_row[...] = filled
    pl.semaphore_wait(barrier, 5)
    for j in range(3):
        c_copy(j).start()
    for j in range(2):
        h_copy(j).start()

    @pl.loop(0, blocks)
    def _(c):
        x_copy(c).start()

    for j in range(8):
        w_copy(j).wait()
        w = summed[j]
        if j < 2:
            w = w * (DIM**-0.5 * math.log2(math.e))
        if j // 2 in (0, 2):
            w = w.T
            where = (pl.ds(j % 2 * rows, rows), slice(None))
        else:
            where = (slice(None), pl.ds(j % 2 * rows, rows))
        high, rest = split(w)
        w_hi[(j // 2, *where)] = high
        w_lo[(j // 2, *where)] = rest

    def low(n):
        return iota((n, PAIR), 1) < DIM

    def mark(n):
        return iota((n, PAIR), 1) == DIM

    def weights(j, p):
        columns = pl.ds(p * rows, rows)
        return w_hi[j, :, columns], w_lo[j, :, columns]

    def project_across(j, xh, xl):
        wh, wl = w_hi[j], w_lo[j]
        return split(dot_nt(wh, xh) + dot_nt(wh, xl) + dot_nt(wl, xh))

    def bias_of(count):
        dead = (iota((BLK, PAIR), 0) >= count) & mark(BLK)
        return jnp.where(dead, MASKED, 0.0)

    def count_in(row, b):
        return jnp.sum(jnp.where(iota(row.shape, 1) == b, row, 0.0), axis=1, keepdims=True).astype(jnp.int32)

    def store_keys(xh, xl, k_ref, v_ref, slots, bias):
        lo = low(rows)
        for p in range(pairs // 2):
            both = dot3(xh, xl, *weights(1, p))
            for half in range(2):
                h = 4 * p + 2 * half
                k = both[:, half * PAIR : (half + 1) * PAIR]
                kh = k.astype(BF16).astype(F32)
                kl = k - kh
                kh_, kl_ = swap(kh), swap(kl)
                for head, a, b in ((h, jnp.where(lo, kh, kl_), kh), (h + 1, jnp.where(lo, kh_, kl), kh_)):
                    a = a.astype(BF16)
                    b = jnp.where(lo, b, bias).astype(BF16)
                    for n, slot in enumerate(slots):
                        k_ref[slot, head, :, :PAIR] = a[n * BLK : (n + 1) * BLK]
                        k_ref[slot, head, :, PAIR:] = b[n * BLK : (n + 1) * BLK]
        vh, vl = project_across(2, xh, xl)
        for h in range(HEADS):
            for n, slot in enumerate(slots):
                part = (slice(h * DIM, (h + 1) * DIM), slice(n * BLK, (n + 1) * BLK))
                v_ref[slot, h, :DIM] = vh[part]
                v_ref[slot, h, DIM:] = vl[part]

    def own_group(i):
        own_copy(i).wait()
        xh, xl = split(normalize(own[group_rows(i)], gain[...]))
        q_hi[i], q_lo[i] = project_across(0, xh, xl)
        bias = jnp.concatenate([bias_of(counts[0, 2 * i]), bias_of(counts[0, 2 * i + 1])], axis=0)
        slot = lax.rem(2 * i, RING)
        store_keys(xh, xl, k_ring, v_ring, (slot, slot + 1), bias)

    def halo_group():
        for j in range(2):
            h_copy(j).wait()
            c_copy(j).wait()
        xh, xl = split(normalize(halo[...], gain[...]))
        before = jnp.where(seg == 0, 0, count_in(cnt[0, 0:1], blocks - 1))
        after = jnp.where(seg == segs - 1, 0, count_in(cnt[1, 0:1], 0))
        bias = jnp.concatenate([bias_of(before), bias_of(after)], axis=0)
        store_keys(xh, xl, k_ring, v_ring, (RING - 1, RING), bias)

    use_near = lax.rem(partner[0, 0] + odd, 2) == 1

    def strip_group(i):
        z_copy(2 * i).wait_recv()
        z_copy(2 * i + 1).wait_recv()
        x = jnp.where(use_near, near[group_rows(i)], far[group_rows(i)])
        row = jnp.where(use_near, cnt[2, 0:1], cnt[3, 0:1])
        xh, xl = split(normalize(x, gain[...]))
        bias = jnp.concatenate([bias_of(count_in(row, 2 * i)), bias_of(count_in(row, 2 * i + 1))], axis=0)
        store_keys(xh, xl, k_strip, v_strip, (2 * i, 2 * i + 1), bias)

    def queries(i, h):
        part = slice(h * DIM, (h + 1) * DIM)
        one = jnp.where(iota((DIM, rows), 0) == 0, 1.0, 0.0).astype(BF16)
        return jnp.concatenate([q_hi[i, part], q_hi[i, part], q_lo[i, part], one], axis=0)

    def weigh(s, top, v):
        e = jnp.exp2(s - top)
        both = dot(v, jnp.concatenate(split(e), axis=1))
        both = both[:, :BLK] + both[:, BLK:]
        return both[:DIM] + both[DIM:], jnp.sum(e, axis=0, keepdims=True)

    def local_group(i, last=False):
        slots = [lax.rem(2 * i - 1 + j + RING, RING) for j in range(4)]
        if last:
            slots[3] = RING
        for h in range(HEADS):
            k = jnp.concatenate([k_ring[slot, h] for slot in slots], axis=0)
            v = jnp.concatenate([v_ring[slot, h] for slot in slots], axis=1)
            scores = dot(k, queries(i, h))
            for n in range(2):
                columns = slice(n * BLK, (n + 1) * BLK)
                keys = slice(n * BLK, (n + 3) * BLK)
                s = scores[keys, columns]
                top = jnp.max(s, axis=0, keepdims=True)
                part, total = weigh(s, top, v[:, keys])
                summed[i, h * DIM : (h + 1) * DIM, columns] = part
                tops[i, h : h + 1, columns] = top
                totals[i, h : h + 1, columns] = total

    for h in range(HEADS):
        k_strip[blocks, h, :, :PAIR] = jnp.zeros((BLK, PAIR), BF16)
        k_strip[blocks, h, :, PAIR:] = bias_of(0).astype(BF16)
        v_strip[blocks, h] = jnp.zeros((BLK, PAIR), BF16)

    @pl.loop(0, groups)
    def _(i):
        x_copy(2 * i).wait_recv()
        z_copy(2 * i).start()

        @pl.when(i == 0)
        def _():
            c_copy(2).wait()
            c_copy(3).start()

        own_group(i)
        x_copy(2 * i + 1).wait_recv()
        z_copy(2 * i + 1).start()

        @pl.when(i == 0)
        def _():
            halo_group()
            c_copy(3).wait()

        @pl.when(i > 0)
        def _():
            local_group(i - 1)
            strip_group(i - 1)

    local_group(groups - 1, last=True)
    strip_group(groups - 1)

    @pl.loop(0, groups)
    def _(i):
        picks = [[jnp.where(listed[2 * i + n, j] < 0, blocks, listed[2 * i + n, j]) for j in range(2)] for n in range(2)]
        heads = []
        for h in range(HEADS):
            q = queries(i, h)
            parts = []
            for n in range(2):
                columns = slice(n * BLK, (n + 1) * BLK)
                k = jnp.concatenate([k_strip[pick, h] for pick in picks[n]], axis=0)
                v = jnp.concatenate([v_strip[pick, h] for pick in picks[n]], axis=1)
                s = dot(k, q[:, columns])
                before = tops[i, h : h + 1, columns]
                top = jnp.maximum(jnp.max(s, axis=0, keepdims=True), before)
                part, total = weigh(s, top, v)
                weight = jnp.exp2(before - top)
                total = total + totals[i, h : h + 1, columns] * weight
                part = part + summed[i, h * DIM : (h + 1) * DIM, columns] * weight
                parts.append(part * (1.0 / total))
            heads.append(jnp.concatenate(parts, axis=1))
        ah, al = split(jnp.concatenate(heads, axis=0).T)
        r = group_rows(i)
        row = iota((BLK, 2 * PAIR), 0)
        live = jnp.concatenate([row < counts[0, 2 * i + n] for n in range(2)], axis=0)
        for p in range(pairs // 2):
            columns = slice(p * 2 * PAIR, (p + 1) * 2 * PAIR)
            result = own[r, columns] + dot3(ah, al, *weights(3, p))
            own[r, columns] = jnp.where(live, result, 0.0)
        out_copy(i).start()

    @pl.loop(0, blocks)
    def _(c):
        x_copy(c).wait_send()
        z_copy(c).wait_send()

    for i in range(groups):
        out_copy(i).wait()


def body(feats, norm_gain, w_qkv, w_out, counts, partner, cross_list):
    points = feats[0]
    rows, width = points.shape
    blocks = counts.shape[1]
    groups = blocks // 2
    hbm = pl.BlockSpec(memory_space=pl.ANY)
    vmem = pl.BlockSpec(memory_space=pltpu.VMEM)
    smem = pl.BlockSpec(memory_space=pltpu.SMEM)
    dma = pltpu.SemaphoreType.DMA
    mixed = pl.pallas_call(
        functools.partial(kernel, blocks),
        out_shape=jax.ShapeDtypeStruct((rows, width), F32),
        in_specs=[hbm, vmem, hbm, hbm, smem, smem, smem],
        out_specs=hbm,
        scratch_shapes=[
            pltpu.VMEM((rows, width), F32),
            pltpu.VMEM((rows, width), F32),
            pltpu.VMEM((rows, width), F32),
            pltpu.VMEM((2 * BLK, width), F32),
            pltpu.VMEM((8, BLK), F32),
            pltpu.VMEM((4, 8, BLK), F32),
            pltpu.VMEM((4, width, width), BF16),
            pltpu.VMEM((4, width, width), BF16),
            pltpu.VMEM((groups, width, 2 * BLK), BF16),
            pltpu.VMEM((groups, width, 2 * BLK), BF16),
            pltpu.VMEM((RING + 1, HEADS, BLK, 2 * PAIR), BF16),
            pltpu.VMEM((RING + 1, HEADS, PAIR, BLK), BF16),
            pltpu.VMEM((blocks + 1, HEADS, BLK, 2 * PAIR), BF16),
            pltpu.VMEM((blocks + 1, HEADS, PAIR, BLK), BF16),
            pltpu.VMEM((groups, width, 2 * BLK), F32),
            pltpu.VMEM((groups, HEADS, 2 * BLK), F32),
            pltpu.VMEM((groups, HEADS, 2 * BLK), F32),
            dma((blocks,)), dma((blocks,)), dma((blocks,)), dma((blocks,)),
            dma((2,)), dma((2,)), dma((4,)), dma((4,)),
            dma((groups,)), dma((8,)), dma((groups,)),
        ],
        compiler_params=pltpu.CompilerParams(
            collective_id=0, has_side_effects=True, vmem_limit_bytes=60 * 1024 * 1024
        ),
    )(points, norm_gain.reshape(1, width), w_qkv, w_out, counts, partner, cross_list[0])
    return mixed[None]


def solution(mesh):
    in_specs = (
        P("line", "seg", None),
        P(),
        P(),
        P(),
        P("line", "seg"),
        P("line", "seg"),
        P("line", "seg", None),
    )
    out_specs = P("line", "seg", None)
    return jax.shard_map(body, mesh=mesh, in_specs=in_specs, out_specs=out_specs, check_vma=False)
```

```python
import functools
import math

import jax
import jax.numpy as jnp
from jax import lax
from jax.experimental import pallas as pl
from jax.experimental.pallas import tpu as pltpu
from jax.sharding import PartitionSpec as P

MESH = pl.DeviceIdType.MESH
F32, BF16 = jnp.float32, jnp.bfloat16
HEADS = 8
BLK = 128
DIM = 64
PAIR = 2 * DIM
RING = 8
BATCH = 4
PIPED = True
MASKED = -1e30
NT = (((1,), (1,)), ((), ()))


def split(x):
    high = x.astype(BF16)
    return high, (x - high.astype(F32)).astype(BF16)


def dot(a, b):
    return jnp.dot(a, b, preferred_element_type=F32)


def dot3(ah, al, bh, bl):
    return dot(ah, bh) + dot(al, bh) + dot(ah, bl)


def normalize(x, gain):
    center = x - jnp.mean(x, axis=-1, keepdims=True)
    spread = jnp.mean(center * center, axis=-1, keepdims=True)
    return center * lax.rsqrt(spread + 1e-05) * gain


def iota(shape, dim):
    return lax.broadcasted_iota(jnp.int32, shape, dim)


def dot_nt(a, b):
    return lax.dot_general(a, b, NT, preferred_element_type=F32)


def swap(x):
    return pltpu.roll(x, DIM, 1)


def kernel(
    blocks,
    feats, gain, w_qkv, w_out, counts, partner, listed,
    out,
    own, near, far, halo, counts_row, cnt,
    w_hi, w_lo, q_hi, q_lo, k_ring, v_ring, k_strip, v_strip, summed, tops, totals,
    x_send, x_recv, z_send, z_recv, h_send, h_recv, c_send, c_recv,
    own_sem, w_sem, out_sem,
):
    groups = blocks // 2
    rows = 2 * BLK
    width = own.shape[1]
    pairs = width // PAIR
    line, seg = lax.axis_index("line"), lax.axis_index("seg")
    lines, segs = lax.axis_size("line"), lax.axis_size("seg")
    odd = lax.rem(line, 2)
    mate = line + 1 - 2 * odd
    ahead = lax.rem(line + 2 - 4 * odd + lines, lines)
    behind = lax.rem(line - 2 + 4 * odd + lines, lines)
    right, left = lax.rem(seg + 1, segs), lax.rem(seg + segs - 1, segs)

    def group_rows(i):
        return pl.ds(pl.multiple_of(i * rows, rows), rows)

    def block_rows(b):
        return pl.ds(pl.multiple_of(b * BLK, BLK), BLK)

    def own_copy(i):
        return pltpu.make_async_copy(feats.at[group_rows(i)], own.at[group_rows(i)], own_sem.at[i])

    def w_copy(j):
        source = w_qkv.at[:, pl.ds(j * rows, rows)] if j < 6 else w_out.at[:, pl.ds((j - 6) * rows, rows)]
        return pltpu.make_async_copy(source, summed.at[j], w_sem.at[j])

    def out_copy(i):
        return pltpu.make_async_copy(own.at[group_rows(i)], out.at[group_rows(i)], out_sem.at[i])

    def remote(source, target, send, recv, device):
        return pltpu.make_async_remote_copy(
            src_ref=source, dst_ref=target, send_sem=send, recv_sem=recv,
            device_id=device, device_id_type=MESH,
        )

    def x_copy(c):
        return remote(feats.at[block_rows(c)], near.at[block_rows(c)], x_send.at[c], x_recv.at[c], (mate, seg))

    def z_copy(c):
        return remote(near.at[block_rows(c)], far.at[block_rows(c)], z_send.at[c], z_recv.at[c], (ahead, seg))

    def h_copy(j):
        b, device = ((blocks - 1), (line, right)) if j == 0 else (0, (line, left))
        return remote(feats.at[pl.ds(b * BLK, BLK)], halo.at[pl.ds(j * BLK, BLK)], h_send.at[j], h_recv.at[j], device)

    def c_copy(j):
        source = cnt.at[2] if j == 3 else counts_row
        device = ((line, right), (line, left), (mate, seg), (ahead, seg))[j]
        return remote(source, cnt.at[j], c_send.at[j], c_recv.at[j], device)

    barrier = pltpu.get_barrier_semaphore()
    for device in ((mate, seg), (ahead, seg), (behind, seg), (line, right), (line, left)):
        pl.semaphore_signal(barrier, inc=1, device_id=device, device_id_type=MESH)
    for i in range(groups):
        own_copy(i).start()
    for j in range(8):
        w_copy(j).start()
    lane = iota((8, BLK), 1)
    filled = jnp.zeros((8, BLK), F32)
    for b in range(blocks):
        filled = jnp.where(lane == b, counts[0, b].astype(F32), filled)
    counts_row[...] = filled
    pl.semaphore_wait(barrier, 5)
    for j in range(3):
        c_copy(j).start()
    for j in range(2):
        h_copy(j).start()

    @pl.loop(0, blocks)
    def _(c):
        x_copy(c).start()

    for j in range(8):
        w_copy(j).wait()
        w = summed[j]
        if j < 2:
            w = w * (DIM**-0.5 * math.log2(math.e))
        if j // 2 in (0, 2):
            w = w.T
            where = (pl.ds(j % 2 * rows, rows), slice(None))
        else:
            where = (slice(None), pl.ds(j % 2 * rows, rows))
        high, rest = split(w)
        w_hi[(j // 2, *where)] = high
        w_lo[(j // 2, *where)] = rest

    def low(n):
        return iota((n, PAIR), 1) < DIM

    def mark(n):
        return iota((n, PAIR), 1) == DIM

    def weights(j, p):
        columns = pl.ds(p * rows, rows)
        return w_hi[j, :, columns], w_lo[j, :, columns]

    def project_across(j, xh, xl):
        wh, wl = w_hi[j], w_lo[j]
        return split(dot_nt(wh, xh) + dot_nt(wh, xl) + dot_nt(wl, xh))

    def bias_of(count):
        dead = (iota((BLK, PAIR), 0) >= count) & mark(BLK)
        return jnp.where(dead, MASKED, 0.0)

    def count_in(row, b):
        return jnp.sum(jnp.where(iota(row.shape, 1) == b, row, 0.0), axis=1, keepdims=True).astype(jnp.int32)

    def store_keys(xh, xl, k_ref, v_ref, slots, bias):
        lo = low(rows)
        for p in range(pairs // 2):
            both = dot3(xh, xl, *weights(1, p))
            for half in range(2):
                h = 4 * p + 2 * half
                k = both[:, half * PAIR : (half + 1) * PAIR]
                kh = k.astype(BF16).astype(F32)
                kl = k - kh
                kh_, kl_ = swap(kh), swap(kl)
                for head, a, b in ((h, jnp.where(lo, kh, kl_), kh), (h + 1, jnp.where(lo, kh_, kl), kh_)):
                    a = a.astype(BF16)
                    b = jnp.where(lo, b, bias).astype(BF16)
                    for n, slot in enumerate(slots):
                        k_ref[slot, head, :, :PAIR] = a[n * BLK : (n + 1) * BLK]
                        k_ref[slot, head, :, PAIR:] = b[n * BLK : (n + 1) * BLK]
        vh, vl = project_across(2, xh, xl)
        for h in range(HEADS):
            for n, slot in enumerate(slots):
                part = (slice(h * DIM, (h + 1) * DIM), slice(n * BLK, (n + 1) * BLK))
                v_ref[slot, h, :DIM] = vh[part]
                v_ref[slot, h, DIM:] = vl[part]

    def own_group(i):
        own_copy(i).wait()
        xh, xl = split(normalize(own[group_rows(i)], gain[...]))
        q_hi[i], q_lo[i] = project_across(0, xh, xl)
        bias = jnp.concatenate([bias_of(counts[0, 2 * i]), bias_of(counts[0, 2 * i + 1])], axis=0)
        slot = lax.rem(2 * i, RING)
        store_keys(xh, xl, k_ring, v_ring, (slot, slot + 1), bias)

    def halo_group():
        for j in range(2):
            h_copy(j).wait()
            c_copy(j).wait()
        xh, xl = split(normalize(halo[...], gain[...]))
        before = jnp.where(seg == 0, 0, count_in(cnt[0, 0:1], blocks - 1))
        after = jnp.where(seg == segs - 1, 0, count_in(cnt[1, 0:1], 0))
        bias = jnp.concatenate([bias_of(before), bias_of(after)], axis=0)
        store_keys(xh, xl, k_ring, v_ring, (RING - 1, RING), bias)

    use_near = lax.rem(partner[0, 0] + odd, 2) == 1

    def strip_group(i):
        z_copy(2 * i).wait_recv()
        z_copy(2 * i + 1).wait_recv()
        x = jnp.where(use_near, near[group_rows(i)], far[group_rows(i)])
        row = jnp.where(use_near, cnt[2, 0:1], cnt[3, 0:1])
        xh, xl = split(normalize(x, gain[...]))
        bias = jnp.concatenate([bias_of(count_in(row, 2 * i)), bias_of(count_in(row, 2 * i + 1))], axis=0)
        store_keys(xh, xl, k_strip, v_strip, (2 * i, 2 * i + 1), bias)

    def queries(i, h):
        part = slice(h * DIM, (h + 1) * DIM)
        one = jnp.where(iota((DIM, rows), 0) == 0, 1.0, 0.0).astype(BF16)
        return jnp.concatenate([q_hi[i, part], q_hi[i, part], q_lo[i, part], one], axis=0)

    def tiled(x):
        return x.reshape(-1, 8, BLK)

    def over_rows(reduce, x):
        return jnp.broadcast_to(reduce(reduce(tiled(x), axis=0), axis=0, keepdims=True), (8, BLK))

    halves = [slice(n * BLK, (n + 1) * BLK) for n in range(2)]

    def attend(score, values, floor, finish):
        batches = [range(h, h + BATCH) for h in range(0, HEADS, BATCH)]
        scores = [score(h) for h in batches[0]]
        for number, batch in enumerate(batches):
            items = [(h, n) for h in batch for n in range(2)]
            flat = [s for pair in scores for s in pair]
            if PIPED and number + 1 < len(batches):
                scores = [score(h) for h in batches[number + 1]]
            peaks = [over_rows(jnp.max, s) for s in flat]
            peaks = [floor(h, n, top) for (h, n), top in zip(items, peaks)]
            powers = [jnp.exp2(tiled(s) - top).reshape(s.shape) for s, top in zip(flat, peaks)]
            sums = [over_rows(jnp.sum, e) for e in powers]
            products = [dot(values(h, n), jnp.concatenate(split(e), axis=1)) for (h, n), e in zip(items, powers)]
            if not PIPED and number + 1 < len(batches):
                scores = [score(h) for h in batches[number + 1]]
            for (h, n), both, total, top in zip(items, products, sums, peaks):
                both = both[:, :BLK] + both[:, BLK:]
                finish(h, n, both[:DIM] + both[DIM:], total, top)

    def local_group(i, last=False):
        slots = [lax.rem(2 * i - 1 + j + RING, RING) for j in range(4)]
        if last:
            slots[3] = RING

        def score(h):
            k = jnp.concatenate([k_ring[slot, h] for slot in slots], axis=0)
            s = dot(k, queries(i, h))
            return [s[n * BLK : (n + 3) * BLK, halves[n]] for n in range(2)]

        def values(h, n):
            return jnp.concatenate([v_ring[slot, h] for slot in slots[n : n + 3]], axis=1)

        def finish(h, n, part, total, top):
            summed[i, h * DIM : (h + 1) * DIM, halves[n]] = part
            tops[i, h, :, halves[n]] = top
            totals[i, h, :, halves[n]] = total

        attend(score, values, lambda h, n, top: top, finish)

    for h in range(HEADS):
        k_strip[blocks, h, :, :PAIR] = jnp.zeros((BLK, PAIR), BF16)
        k_strip[blocks, h, :, PAIR:] = bias_of(0).astype(BF16)
        v_strip[blocks, h] = jnp.zeros((BLK, PAIR), BF16)

    @pl.loop(0, groups)
    def _(i):
        x_copy(2 * i).wait_recv()
        z_copy(2 * i).start()

        @pl.when(i == 0)
        def _():
            c_copy(2).wait()
            c_copy(3).start()

        own_group(i)
        x_copy(2 * i + 1).wait_recv()
        z_copy(2 * i + 1).start()

        @pl.when(i == 0)
        def _():
            halo_group()
            c_copy(3).wait()

        @pl.when(i > 0)
        def _():
            local_group(i - 1)
            strip_group(i - 1)

    local_group(groups - 1, last=True)
    strip_group(groups - 1)

    @pl.loop(0, groups)
    def _(i):
        picks = [[jnp.where(listed[2 * i + n, j] < 0, blocks, listed[2 * i + n, j]) for j in range(2)] for n in range(2)]
        heads = {}

        def score(h):
            q = queries(i, h)
            return [dot(jnp.concatenate([k_strip[pick, h] for pick in picks[n]], axis=0), q[:, halves[n]]) for n in range(2)]

        def values(h, n):
            return jnp.concatenate([v_strip[pick, h] for pick in picks[n]], axis=1)

        def floor(h, n, top):
            return jnp.maximum(top, tops[i, h, :, halves[n]])

        def finish(h, n, part, total, top):
            weight = jnp.exp2(tops[i, h, :, halves[n]] - top)
            total = total + totals[i, h, :, halves[n]] * weight
            part = tiled(part) + tiled(summed[i, h * DIM : (h + 1) * DIM, halves[n]]) * weight
            heads[h, n] = (part * (1.0 / total)).reshape(DIM, BLK)

        attend(score, values, floor, finish)
        heads = [jnp.concatenate([heads[h, 0], heads[h, 1]], axis=1) for h in range(HEADS)]
        ah, al = split(jnp.concatenate(heads, axis=0).T)
        r = group_rows(i)
        row = iota((BLK, 2 * PAIR), 0)
        live = jnp.concatenate([row < counts[0, 2 * i + n] for n in range(2)], axis=0)
        for p in range(pairs // 2):
            columns = slice(p * 2 * PAIR, (p + 1) * 2 * PAIR)
            result = own[r, columns] + dot3(ah, al, *weights(3, p))
            own[r, columns] = jnp.where(live, result, 0.0)
        out_copy(i).start()

    @pl.loop(0, blocks)
    def _(c):
        x_copy(c).wait_send()
        z_copy(c).wait_send()

    for i in range(groups):
        out_copy(i).wait()


def body(feats, norm_gain, w_qkv, w_out, counts, partner, cross_list):
    points = feats[0]
    rows, width = points.shape
    blocks = counts.shape[1]
    groups = blocks // 2
    hbm = pl.BlockSpec(memory_space=pl.ANY)
    vmem = pl.BlockSpec(memory_space=pltpu.VMEM)
    smem = pl.BlockSpec(memory_space=pltpu.SMEM)
    dma = pltpu.SemaphoreType.DMA
    mixed = pl.pallas_call(
        functools.partial(kernel, blocks),
        out_shape=jax.ShapeDtypeStruct((rows, width), F32),
        in_specs=[hbm, vmem, hbm, hbm, smem, smem, smem],
        out_specs=hbm,
        scratch_shapes=[
            pltpu.VMEM((rows, width), F32),
            pltpu.VMEM((rows, width), F32),
            pltpu.VMEM((rows, width), F32),
            pltpu.VMEM((2 * BLK, width), F32),
            pltpu.VMEM((8, BLK), F32),
            pltpu.VMEM((4, 8, BLK), F32),
            pltpu.VMEM((4, width, width), BF16),
            pltpu.VMEM((4, width, width), BF16),
            pltpu.VMEM((groups, width, 2 * BLK), BF16),
            pltpu.VMEM((groups, width, 2 * BLK), BF16),
            pltpu.VMEM((RING + 1, HEADS, BLK, 2 * PAIR), BF16),
            pltpu.VMEM((RING + 1, HEADS, PAIR, BLK), BF16),
            pltpu.VMEM((blocks + 1, HEADS, BLK, 2 * PAIR), BF16),
            pltpu.VMEM((blocks + 1, HEADS, PAIR, BLK), BF16),
            pltpu.VMEM((groups, width, 2 * BLK), F32),
            pltpu.VMEM((groups, HEADS, 8, 2 * BLK), F32),
            pltpu.VMEM((groups, HEADS, 8, 2 * BLK), F32),
            dma((blocks,)), dma((blocks,)), dma((blocks,)), dma((blocks,)),
            dma((2,)), dma((2,)), dma((4,)), dma((4,)),
            dma((groups,)), dma((8,)), dma((groups,)),
        ],
        compiler_params=pltpu.CompilerParams(
            collective_id=0, has_side_effects=True, vmem_limit_bytes=60 * 1024 * 1024
        ),
    )(points, norm_gain.reshape(1, width), w_qkv, w_out, counts, partner, cross_list[0])
    return mixed[None]


def solution(mesh):
    in_specs = (
        P("line", "seg", None),
        P(),
        P(),
        P(),
        P("line", "seg"),
        P("line", "seg"),
        P("line", "seg", None),
    )
    out_specs = P("line", "seg", None)
    return jax.shard_map(body, mesh=mesh, in_specs=in_specs, out_specs=out_specs, check_vma=False)
```

```python
import functools
import math

import jax
import jax.numpy as jnp
from jax import lax
from jax.experimental import pallas as pl
from jax.experimental.pallas import tpu as pltpu
from jax.sharding import PartitionSpec as P

MESH = pl.DeviceIdType.MESH
F32, BF16 = jnp.float32, jnp.bfloat16
HEADS = 8
BLK = 128
DIM = 64
PAIR = 2 * DIM
CHUNK = 64
BATCH = 4
PIPED = True
MASKED = -1e30
NT = (((1,), (1,)), ((), ()))


def split(x):
    high = x.astype(BF16)
    return high, (x - high.astype(F32)).astype(BF16)


def dot(a, b):
    return jnp.dot(a, b, preferred_element_type=F32)


def dot3(ah, al, bh, bl):
    return dot(ah, bh) + dot(al, bh) + dot(ah, bl)


def normalize(x, gain):
    center = x - jnp.mean(x, axis=-1, keepdims=True)
    spread = jnp.mean(center * center, axis=-1, keepdims=True)
    return center * lax.rsqrt(spread + 1e-05) * gain


def iota(shape, dim):
    return lax.broadcasted_iota(jnp.int32, shape, dim)


def dot_nt(a, b):
    return lax.dot_general(a, b, NT, preferred_element_type=F32)


def swap(x):
    return pltpu.roll(x, DIM, 1)


def kernel(
    blocks,
    feats, gain, w_qkv, w_out, counts, partner, listed,
    out,
    own, near, far, halo, counts_row, cnt,
    w_hi, w_lo, q_hi, q_lo, k_own, v_own, k_strip, v_strip, summed, tops, totals,
    x_send, x_recv, z_send, z_recv, h_send, h_recv, c_send, c_recv,
    own_sem, w_sem, out_sem,
):
    groups = blocks // 2
    rows = 2 * BLK
    each = rows // CHUNK
    width = own.shape[1]
    pairs = width // PAIR
    line, seg = lax.axis_index("line"), lax.axis_index("seg")
    lines, segs = lax.axis_size("line"), lax.axis_size("seg")
    odd = lax.rem(line, 2)
    mate = line + 1 - 2 * odd
    ahead = lax.rem(line + 2 - 4 * odd + lines, lines)
    behind = lax.rem(line - 2 + 4 * odd + lines, lines)
    right, left = lax.rem(seg + 1, segs), lax.rem(seg + segs - 1, segs)

    def group_rows(i):
        return pl.ds(pl.multiple_of(i * rows, rows), rows)

    def chunk_rows(c):
        return pl.ds(pl.multiple_of(c * CHUNK, CHUNK), CHUNK)

    def own_copy(i):
        return pltpu.make_async_copy(feats.at[group_rows(i)], own.at[group_rows(i)], own_sem.at[i])

    def w_copy(j):
        source = w_qkv.at[:, pl.ds(j * rows, rows)] if j < 6 else w_out.at[:, pl.ds((j - 6) * rows, rows)]
        return pltpu.make_async_copy(source, summed.at[j], w_sem.at[j])

    def out_copy(i):
        return pltpu.make_async_copy(own.at[group_rows(i)], out.at[group_rows(i)], out_sem.at[i])

    def remote(source, target, send, recv, device):
        return pltpu.make_async_remote_copy(
            src_ref=source, dst_ref=target, send_sem=send, recv_sem=recv,
            device_id=device, device_id_type=MESH,
        )

    def x_copy(c):
        return remote(feats.at[chunk_rows(c)], near.at[chunk_rows(c)], x_send.at[c], x_recv.at[c], (mate, seg))

    def z_copy(c):
        return remote(near.at[chunk_rows(c)], far.at[chunk_rows(c)], z_send.at[c], z_recv.at[c], (ahead, seg))

    def h_copy(j):
        b, device = ((blocks - 1), (line, right)) if j == 0 else (0, (line, left))
        return remote(feats.at[pl.ds(b * BLK, BLK)], halo.at[pl.ds(j * BLK, BLK)], h_send.at[j], h_recv.at[j], device)

    def c_copy(j):
        source = cnt.at[2] if j == 3 else counts_row
        device = ((line, right), (line, left), (mate, seg), (ahead, seg))[j]
        return remote(source, cnt.at[j], c_send.at[j], c_recv.at[j], device)

    barrier = pltpu.get_barrier_semaphore()
    for device in ((mate, seg), (ahead, seg), (behind, seg), (line, right), (line, left)):
        pl.semaphore_signal(barrier, inc=1, device_id=device, device_id_type=MESH)
    for i in range(groups):
        own_copy(i).start()
    for j in range(8):
        w_copy(j).start()
    lane = iota((8, BLK), 1)
    filled = jnp.zeros((8, BLK), F32)
    for b in range(blocks):
        filled = jnp.where(lane == b, counts[0, b].astype(F32), filled)
    counts_row[...] = filled
    pl.semaphore_wait(barrier, 5)
    for j in range(3):
        c_copy(j).start()
    for j in range(2):
        h_copy(j).start()

    @pl.loop(0, groups * each)
    def _(c):
        x_copy(c).start()

    for j in range(8):
        w_copy(j).wait()
        w = summed[j]
        if j < 2:
            w = w * (DIM**-0.5 * math.log2(math.e))
        if j // 2 in (0, 2):
            w = w.T
            where = (pl.ds(j % 2 * rows, rows), slice(None))
        else:
            where = (slice(None), pl.ds(j % 2 * rows, rows))
        high, rest = split(w)
        w_hi[(j // 2, *where)] = high
        w_lo[(j // 2, *where)] = rest

    def low(n):
        return iota((n, PAIR), 1) < DIM

    def mark(n):
        return iota((n, PAIR), 1) == DIM

    def weights(j, p):
        columns = pl.ds(p * rows, rows)
        return w_hi[j, :, columns], w_lo[j, :, columns]

    def project_across(j, xh, xl):
        wh, wl = w_hi[j], w_lo[j]
        return split(dot_nt(wh, xh) + dot_nt(wh, xl) + dot_nt(wl, xh))

    def bias_of(count):
        dead = (iota((BLK, PAIR), 0) >= count) & mark(BLK)
        return jnp.where(dead, MASKED, 0.0)

    def count_in(row, b):
        return jnp.sum(jnp.where(iota(row.shape, 1) == b, row, 0.0), axis=1, keepdims=True).astype(jnp.int32)

    def store_keys(xh, xl, k_ref, v_ref, slots, bias):
        lo = low(rows)
        for p in range(pairs // 2):
            both = dot3(xh, xl, *weights(1, p))
            for half in range(2):
                h = 4 * p + 2 * half
                k = both[:, half * PAIR : (half + 1) * PAIR]
                kh = k.astype(BF16).astype(F32)
                kl = k - kh
                kh_, kl_ = swap(kh), swap(kl)
                for head, a, b in ((h, jnp.where(lo, kh, kl_), kh), (h + 1, jnp.where(lo, kh_, kl), kh_)):
                    a = a.astype(BF16)
                    b = jnp.where(lo, b, bias).astype(BF16)
                    for n, slot in enumerate(slots):
                        k_ref[slot, head, :, :PAIR] = a[n * BLK : (n + 1) * BLK]
                        k_ref[slot, head, :, PAIR:] = b[n * BLK : (n + 1) * BLK]
        vh, vl = project_across(2, xh, xl)
        for h in range(HEADS):
            for n, slot in enumerate(slots):
                part = (slice(h * DIM, (h + 1) * DIM), slice(n * BLK, (n + 1) * BLK))
                v_ref[slot, h, :DIM] = vh[part]
                v_ref[slot, h, DIM:] = vl[part]

    def own_group(i):
        own_copy(i).wait()
        xh, xl = split(normalize(own[group_rows(i)], gain[...]))
        q_hi[i], q_lo[i] = project_across(0, xh, xl)
        bias = jnp.concatenate([bias_of(counts[0, 2 * i]), bias_of(counts[0, 2 * i + 1])], axis=0)
        store_keys(xh, xl, k_own, v_own, (2 * i, 2 * i + 1), bias)

    def halo_group():
        for j in range(2):
            h_copy(j).wait()
            c_copy(j).wait()
        xh, xl = split(normalize(halo[...], gain[...]))
        before = jnp.where(seg == 0, 0, count_in(cnt[0, 0:1], blocks - 1))
        after = jnp.where(seg == segs - 1, 0, count_in(cnt[1, 0:1], 0))
        bias = jnp.concatenate([bias_of(before), bias_of(after)], axis=0)
        store_keys(xh, xl, k_own, v_own, (blocks - 1, blocks), bias)

    use_near = lax.rem(partner[0, 0] + odd, 2) == 1

    def strip_group(i):
        for n in range(each):
            z_copy(each * i + n).wait_recv()
        x = jnp.where(use_near, near[group_rows(i)], far[group_rows(i)])
        row = jnp.where(use_near, cnt[2, 0:1], cnt[3, 0:1])
        xh, xl = split(normalize(x, gain[...]))
        bias = jnp.concatenate([bias_of(count_in(row, 2 * i)), bias_of(count_in(row, 2 * i + 1))], axis=0)
        store_keys(xh, xl, k_strip, v_strip, (2 * i, 2 * i + 1), bias)

    def queries(i, h):
        part = slice(h * DIM, (h + 1) * DIM)
        one = jnp.where(iota((DIM, rows), 0) == 0, 1.0, 0.0).astype(BF16)
        return jnp.concatenate([q_hi[i, part], q_hi[i, part], q_lo[i, part], one], axis=0)

    def tiled(x):
        return x.reshape(-1, 8, BLK)

    def over_rows(reduce, x):
        return jnp.broadcast_to(reduce(reduce(tiled(x), axis=0), axis=0, keepdims=True), (8, BLK))

    halves = [slice(n * BLK, (n + 1) * BLK) for n in range(2)]

    def attend(score, values, floor, finish):
        batches = [range(h, h + BATCH) for h in range(0, HEADS, BATCH)]
        scores = [score(h) for h in batches[0]]
        for number, batch in enumerate(batches):
            items = [(h, n) for h in batch for n in range(2)]
            flat = [s for pair in scores for s in pair]
            if PIPED and number + 1 < len(batches):
                scores = [score(h) for h in batches[number + 1]]
            peaks = [over_rows(jnp.max, s) for s in flat]
            peaks = [floor(h, n, top) for (h, n), top in zip(items, peaks)]
            powers = [jnp.exp2(tiled(s) - top).reshape(s.shape) for s, top in zip(flat, peaks)]
            sums = [over_rows(jnp.sum, e) for e in powers]
            products = [dot(values(h, n), jnp.concatenate(split(e), axis=1)) for (h, n), e in zip(items, powers)]
            if not PIPED and number + 1 < len(batches):
                scores = [score(h) for h in batches[number + 1]]
            for (h, n), both, total, top in zip(items, products, sums, peaks):
                both = both[:, :BLK] + both[:, BLK:]
                finish(h, n, both[:DIM] + both[DIM:], total, top)

    def local_group(i, last=False):
        slots = [lax.rem(2 * i - 1 + j + blocks, blocks) for j in range(4)]
        if last:
            slots[3] = blocks

        def score(h):
            k = jnp.concatenate([k_own[slot, h] for slot in slots], axis=0)
            s = dot(k, queries(i, h))
            return [s[n * BLK : (n + 3) * BLK, halves[n]] for n in range(2)]

        def values(h, n):
            return jnp.concatenate([v_own[slot, h] for slot in slots[n : n + 3]], axis=1)

        def finish(h, n, part, total, top):
            summed[i, h * DIM : (h + 1) * DIM, halves[n]] = part
            tops[i, h, :, halves[n]] = top
            totals[i, h, :, halves[n]] = total

        attend(score, values, lambda h, n, top: top, finish)

    for h in range(HEADS):
        k_strip[blocks, h, :, :PAIR] = jnp.zeros((BLK, PAIR), BF16)
        k_strip[blocks, h, :, PAIR:] = bias_of(0).astype(BF16)
        v_strip[blocks, h] = jnp.zeros((BLK, PAIR), BF16)

    def pass_on(c):
        x_copy(c).wait_recv()
        z_copy(c).start()

    half = groups // 2

    @pl.loop(0, groups)
    def _(j):
        pass_on(each * j)

        @pl.when(j == 0)
        def _():
            c_copy(2).wait()
            c_copy(3).start()

        @pl.when(j < half)
        def _():
            own_group(2 * j)

        pass_on(each * j + 1)

        @pl.when(j < half)
        def _():
            own_group(2 * j + 1)

        @pl.when(j == 0)
        def _():
            halo_group()
            c_copy(3).wait()

        pass_on(each * j + 2)

        @pl.when((j >= 1) & (j <= half))
        def _():
            local_group(2 * j - 2)

        pass_on(each * j + 3)

        @pl.when((j >= 1) & (j < half))
        def _():
            local_group(2 * j - 1)

        @pl.when(j == half)
        def _():
            local_group(groups - 1, last=True)

        @pl.when(j >= 1)
        def _():
            strip_group(j - 1)

    strip_group(groups - 1)

    @pl.loop(0, groups)
    def _(i):
        picks = [[jnp.where(listed[j, 2 * i + n] < 0, blocks, listed[j, 2 * i + n]) for j in range(2)] for n in range(2)]
        heads = {}

        def score(h):
            q = queries(i, h)
            return [dot(jnp.concatenate([k_strip[pick, h] for pick in picks[n]], axis=0), q[:, halves[n]]) for n in range(2)]

        def values(h, n):
            return jnp.concatenate([v_strip[pick, h] for pick in picks[n]], axis=1)

        def floor(h, n, top):
            return jnp.maximum(top, tops[i, h, :, halves[n]])

        def finish(h, n, part, total, top):
            weight = jnp.exp2(tops[i, h, :, halves[n]] - top)
            total = total + totals[i, h, :, halves[n]] * weight
            part = tiled(part) + tiled(summed[i, h * DIM : (h + 1) * DIM, halves[n]]) * weight
            heads[h, n] = (part * (1.0 / total)).reshape(DIM, BLK)

        attend(score, values, floor, finish)
        heads = [jnp.concatenate([heads[h, 0], heads[h, 1]], axis=1) for h in range(HEADS)]
        ah, al = split(jnp.concatenate(heads, axis=0).T)
        r = group_rows(i)
        row = iota((BLK, 2 * PAIR), 0)
        live = jnp.concatenate([row < counts[0, 2 * i + n] for n in range(2)], axis=0)
        for p in range(pairs // 2):
            columns = slice(p * 2 * PAIR, (p + 1) * 2 * PAIR)
            result = own[r, columns] + dot3(ah, al, *weights(3, p))
            own[r, columns] = jnp.where(live, result, 0.0)
        out_copy(i).start()

    @pl.loop(0, groups * each)
    def _(c):
        x_copy(c).wait_send()
        z_copy(c).wait_send()

    for i in range(groups):
        out_copy(i).wait()


def body(feats, norm_gain, w_qkv, w_out, counts, partner, cross_list):
    points = feats[0]
    rows, width = points.shape
    blocks = counts.shape[1]
    groups, chunks = blocks // 2, rows // CHUNK
    hbm = pl.BlockSpec(memory_space=pl.ANY)
    vmem = pl.BlockSpec(memory_space=pltpu.VMEM)
    smem = pl.BlockSpec(memory_space=pltpu.SMEM)
    dma = pltpu.SemaphoreType.DMA
    mixed = pl.pallas_call(
        functools.partial(kernel, blocks),
        out_shape=jax.ShapeDtypeStruct((rows, width), F32),
        in_specs=[hbm, vmem, hbm, hbm, smem, smem, smem],
        out_specs=hbm,
        scratch_shapes=[
            pltpu.VMEM((rows, width), F32),
            pltpu.VMEM((rows, width), F32),
            pltpu.VMEM((rows, width), F32),
            pltpu.VMEM((2 * BLK, width), F32),
            pltpu.VMEM((8, BLK), F32),
            pltpu.VMEM((4, 8, BLK), F32),
            pltpu.VMEM((4, width, width), BF16),
            pltpu.VMEM((4, width, width), BF16),
            pltpu.VMEM((groups, width, 2 * BLK), BF16),
            pltpu.VMEM((groups, width, 2 * BLK), BF16),
            pltpu.VMEM((blocks + 1, HEADS, BLK, 2 * PAIR), BF16),
            pltpu.VMEM((blocks + 1, HEADS, PAIR, BLK), BF16),
            pltpu.VMEM((blocks + 1, HEADS, BLK, 2 * PAIR), BF16),
            pltpu.VMEM((blocks + 1, HEADS, PAIR, BLK), BF16),
            pltpu.VMEM((groups, width, 2 * BLK), F32),
            pltpu.VMEM((groups, HEADS, 8, 2 * BLK), F32),
            pltpu.VMEM((groups, HEADS, 8, 2 * BLK), F32),
            dma((chunks,)), dma((chunks,)), dma((chunks,)), dma((chunks,)),
            dma((2,)), dma((2,)), dma((4,)), dma((4,)),
            dma((groups,)), dma((8,)), dma((groups,)),
        ],
        compiler_params=pltpu.CompilerParams(
            collective_id=0, has_side_effects=True, vmem_limit_bytes=60 * 1024 * 1024
        ),
    )(points, norm_gain.reshape(1, width), w_qkv, w_out, counts, partner, cross_list[0].T)
    return mixed[None]


def solution(mesh):
    in_specs = (
        P("line", "seg", None),
        P(),
        P(),
        P(),
        P("line", "seg"),
        P("line", "seg"),
        P("line", "seg", None),
    )
    out_specs = P("line", "seg", None)
    return jax.shard_map(body, mesh=mesh, in_specs=in_specs, out_specs=out_specs, check_vma=False)
```

```python
import functools
import math

import jax
import jax.numpy as jnp
from jax import lax
from jax.experimental import pallas as pl
from jax.experimental.pallas import tpu as pltpu
from jax.sharding import PartitionSpec as P

MESH = pl.DeviceIdType.MESH
F32, BF16 = jnp.float32, jnp.bfloat16
HEADS = 8
BLK = 128
DIM = 64
PAIR = 2 * DIM
CHUNK = 64
LATE = 4
BATCH = 4
PIPED = True
MASKED = -1e30
NT = (((1,), (1,)), ((), ()))


def split(x):
    high = x.astype(BF16)
    return high, (x - high.astype(F32)).astype(BF16)


def dot(a, b):
    return jnp.dot(a, b, preferred_element_type=F32)


def dot3(ah, al, bh, bl):
    return dot(ah, bh) + dot(al, bh) + dot(ah, bl)


def normalize(x, gain):
    center = x - jnp.mean(x, axis=-1, keepdims=True)
    spread = jnp.mean(center * center, axis=-1, keepdims=True)
    return center * lax.rsqrt(spread + 1e-05) * gain


def iota(shape, dim):
    return lax.broadcasted_iota(jnp.int32, shape, dim)


def dot_nt(a, b):
    return lax.dot_general(a, b, NT, preferred_element_type=F32)


def swap(x):
    return pltpu.roll(x, DIM, 1)


def tiled(x):
    return x.reshape(-1, 8, BLK)


def over_rows(reduce, x):
    return jnp.broadcast_to(reduce(reduce(tiled(x), axis=0), axis=0, keepdims=True), (8, BLK))


def attend(score, values, floor, finish, parts):
    size = 2 * BATCH // parts
    batches = [range(h, h + size) for h in range(0, HEADS, size)]
    scores = [score(h) for h in batches[0]]
    for number, batch in enumerate(batches):
        items = [(h, n) for h in batch for n in range(parts)]
        flat = [s for pair in scores for s in pair]
        if PIPED and number + 1 < len(batches):
            scores = [score(h) for h in batches[number + 1]]
        peaks = [over_rows(jnp.max, s) for s in flat]
        peaks = [floor(h, n, top) for (h, n), top in zip(items, peaks)]
        powers = [jnp.exp2(tiled(s) - top).reshape(s.shape) for s, top in zip(flat, peaks)]
        sums = [over_rows(jnp.sum, e) for e in powers]
        products = [dot(values(h, n), jnp.concatenate(split(e), axis=1)) for (h, n), e in zip(items, powers)]
        if not PIPED and number + 1 < len(batches):
            scores = [score(h) for h in batches[number + 1]]
        for (h, n), both, total, top in zip(items, products, sums, peaks):
            both = both[:, :BLK] + both[:, BLK:]
            finish(h, n, both[:DIM] + both[DIM:], total, top)


def queries_of(high, low):
    one = jnp.where(iota(high.shape, 0) == 0, 1.0, 0.0).astype(BF16)
    return jnp.concatenate([high, high, low, one], axis=0)


def kernel(
    blocks,
    feats, gain, w_qkv, w_out, counts, partner, listed,
    summed_out, tops_out, totals_out, q_hi_out, q_lo_out, k_out, v_out, w_hi_out, w_lo_out,
    own, near, far, halo, counts_row, cnt,
    w_hi, w_lo, q_hi, q_lo, k_own, v_own, k_strip, v_strip, summed, tops, totals,
    x_send, x_recv, z_send, z_recv, h_send, h_recv, c_send, c_recv,
    own_sem, w_sem, s_sem, q_sem, k_sem, p_sem,
):
    groups = blocks // 2
    rows = 2 * BLK
    each = rows // CHUNK
    width = own.shape[1]
    pairs = width // PAIR
    line, seg = lax.axis_index("line"), lax.axis_index("seg")
    lines, segs = lax.axis_size("line"), lax.axis_size("seg")
    odd = lax.rem(line, 2)
    mate = line + 1 - 2 * odd
    ahead = lax.rem(line + 2 - 4 * odd + lines, lines)
    behind = lax.rem(line - 2 + 4 * odd + lines, lines)
    right, left = lax.rem(seg + 1, segs), lax.rem(seg + segs - 1, segs)

    def group_rows(i):
        return pl.ds(pl.multiple_of(i * rows, rows), rows)

    def chunk_rows(c):
        return pl.ds(pl.multiple_of(c * CHUNK, CHUNK), CHUNK)

    def own_copy(i):
        return pltpu.make_async_copy(feats.at[group_rows(i)], own.at[group_rows(i)], own_sem.at[i])

    def w_copy(j):
        source = w_qkv.at[:, pl.ds(j * rows, rows)] if j < 6 else w_out.at[:, pl.ds((j - 6) * rows, rows)]
        return pltpu.make_async_copy(source, summed.at[j], w_sem.at[j])

    def sums_out(i):
        pairs_ = ((summed, summed_out), (tops, tops_out), (totals, totals_out))
        return [pltpu.make_async_copy(a.at[i], b.at[i], s_sem.at[n, i]) for n, (a, b) in enumerate(pairs_)]

    def queries_out(i):
        pairs_ = ((q_hi, q_hi_out), (q_lo, q_lo_out))
        return [pltpu.make_async_copy(a.at[i], b.at[i], q_sem.at[n, i]) for n, (a, b) in enumerate(pairs_)]

    def keys_out(n):
        source = pl.ds(blocks - LATE + 2 * n, 2 + n)
        target = pl.ds(2 * n, 2 + n)
        return [pltpu.make_async_copy(a.at[source], b.at[target], k_sem.at[m, n]) for m, (a, b) in enumerate(((k_strip, k_out), (v_strip, v_out)))]

    def projection_out():
        return [pltpu.make_async_copy(a.at[3], b, p_sem.at[m]) for m, (a, b) in enumerate(((w_hi, w_hi_out), (w_lo, w_lo_out)))]

    def remote(source, target, send, recv, device):
        return pltpu.make_async_remote_copy(
            src_ref=source, dst_ref=target, send_sem=send, recv_sem=recv,
            device_id=device, device_id_type=MESH,
        )

    def x_copy(c):
        return remote(feats.at[chunk_rows(c)], near.at[chunk_rows(c)], x_send.at[c], x_recv.at[c], (mate, seg))

    def z_copy(c):
        return remote(near.at[chunk_rows(c)], far.at[chunk_rows(c)], z_send.at[c], z_recv.at[c], (ahead, seg))

    def h_copy(j):
        b, device = ((blocks - 1), (line, right)) if j == 0 else (0, (line, left))
        return remote(feats.at[pl.ds(b * BLK, BLK)], halo.at[pl.ds(j * BLK, BLK)], h_send.at[j], h_recv.at[j], device)

    def c_copy(j):
        source = cnt.at[2] if j == 3 else counts_row
        device = ((line, right), (line, left), (mate, seg), (ahead, seg))[j]
        return remote(source, cnt.at[j], c_send.at[j], c_recv.at[j], device)

    barrier = pltpu.get_barrier_semaphore()
    for device in ((mate, seg), (ahead, seg), (behind, seg), (line, right), (line, left)):
        pl.semaphore_signal(barrier, inc=1, device_id=device, device_id_type=MESH)
    for i in range(groups):
        own_copy(i).start()
    for j in range(8):
        w_copy(j).start()
    lane = iota((8, BLK), 1)
    filled = jnp.zeros((8, BLK), F32)
    for b in range(blocks):
        filled = jnp.where(lane == b, counts[0, b].astype(F32), filled)
    counts_row[...] = filled
    pl.semaphore_wait(barrier, 5)
    for j in range(3):
        c_copy(j).start()
    for j in range(2):
        h_copy(j).start()

    @pl.loop(0, groups * each)
    def _(c):
        x_copy(c).start()

    for j in range(8):
        w_copy(j).wait()
        w = summed[j]
        if j < 2:
            w = w * (DIM**-0.5 * math.log2(math.e))
        if j // 2 in (0, 2):
            w = w.T
            where = (pl.ds(j % 2 * rows, rows), slice(None))
        else:
            where = (slice(None), pl.ds(j % 2 * rows, rows))
        high, rest = split(w)
        w_hi[(j // 2, *where)] = high
        w_lo[(j // 2, *where)] = rest

    def low(n):
        return iota((n, PAIR), 1) < DIM

    def mark(n):
        return iota((n, PAIR), 1) == DIM

    def weights(j, p):
        columns = pl.ds(p * rows, rows)
        return w_hi[j, :, columns], w_lo[j, :, columns]

    def project_across(j, xh, xl):
        wh, wl = w_hi[j], w_lo[j]
        return split(dot_nt(wh, xh) + dot_nt(wh, xl) + dot_nt(wl, xh))

    def bias_of(count):
        dead = (iota((BLK, PAIR), 0) >= count) & mark(BLK)
        return jnp.where(dead, MASKED, 0.0)

    def count_in(row, b):
        return jnp.sum(jnp.where(iota(row.shape, 1) == b, row, 0.0), axis=1, keepdims=True).astype(jnp.int32)

    def store_keys(xh, xl, k_ref, v_ref, slots, bias):
        lo = low(rows)
        for p in range(pairs // 2):
            both = dot3(xh, xl, *weights(1, p))
            for half in range(2):
                h = 4 * p + 2 * half
                k = both[:, half * PAIR : (half + 1) * PAIR]
                kh = k.astype(BF16).astype(F32)
                kl = k - kh
                kh_, kl_ = swap(kh), swap(kl)
                for head, a, b in ((h, jnp.where(lo, kh, kl_), kh), (h + 1, jnp.where(lo, kh_, kl), kh_)):
                    a = a.astype(BF16)
                    b = jnp.where(lo, b, bias).astype(BF16)
                    for n, slot in enumerate(slots):
                        k_ref[slot, head, :, :PAIR] = a[n * BLK : (n + 1) * BLK]
                        k_ref[slot, head, :, PAIR:] = b[n * BLK : (n + 1) * BLK]
        vh, vl = project_across(2, xh, xl)
        for h in range(HEADS):
            for n, slot in enumerate(slots):
                part = (slice(h * DIM, (h + 1) * DIM), slice(n * BLK, (n + 1) * BLK))
                v_ref[slot, h, :DIM] = vh[part]
                v_ref[slot, h, DIM:] = vl[part]

    def own_group(i):
        own_copy(i).wait()
        xh, xl = split(normalize(own[group_rows(i)], gain[...]))
        q_hi[i], q_lo[i] = project_across(0, xh, xl)
        for copy in queries_out(i):
            copy.start()
        bias = jnp.concatenate([bias_of(counts[0, 2 * i]), bias_of(counts[0, 2 * i + 1])], axis=0)
        store_keys(xh, xl, k_own, v_own, (2 * i, 2 * i + 1), bias)

    def halo_group():
        for j in range(2):
            h_copy(j).wait()
            c_copy(j).wait()
        xh, xl = split(normalize(halo[...], gain[...]))
        before = jnp.where(seg == 0, 0, count_in(cnt[0, 0:1], blocks - 1))
        after = jnp.where(seg == segs - 1, 0, count_in(cnt[1, 0:1], 0))
        bias = jnp.concatenate([bias_of(before), bias_of(after)], axis=0)
        store_keys(xh, xl, k_own, v_own, (blocks - 1, blocks), bias)

    use_near = lax.rem(partner[0, 0] + odd, 2) == 1

    def strip_group(i):
        for n in range(each):
            z_copy(each * i + n).wait_recv()
        x = jnp.where(use_near, near[group_rows(i)], far[group_rows(i)])
        row = jnp.where(use_near, cnt[2, 0:1], cnt[3, 0:1])
        xh, xl = split(normalize(x, gain[...]))
        bias = jnp.concatenate([bias_of(count_in(row, 2 * i)), bias_of(count_in(row, 2 * i + 1))], axis=0)
        store_keys(xh, xl, k_strip, v_strip, (2 * i, 2 * i + 1), bias)

    def queries(i, h):
        part = slice(h * DIM, (h + 1) * DIM)
        return queries_of(q_hi[i, part], q_lo[i, part])

    halves = [slice(n * BLK, (n + 1) * BLK) for n in range(2)]

    def local_group(i, last=False):
        slots = [lax.rem(2 * i - 1 + j + blocks, blocks) for j in range(4)]
        if last:
            slots[3] = blocks

        def score(h):
            k = jnp.concatenate([k_own[slot, h] for slot in slots], axis=0)
            s = dot(k, queries(i, h))
            return [s[n * BLK : (n + 3) * BLK, halves[n]] for n in range(2)]

        def values(h, n):
            return jnp.concatenate([v_own[slot, h] for slot in slots[n : n + 3]], axis=1)

        def finish(h, n, part, total, top):
            summed[i, h * DIM : (h + 1) * DIM, halves[n]] = part
            tops[i, h, :, halves[n]] = top
            totals[i, h, :, halves[n]] = total

        attend(score, values, lambda h, n, top: top, finish, 2)

    for h in range(HEADS):
        k_strip[blocks, h, :, :PAIR] = jnp.zeros((BLK, PAIR), BF16)
        k_strip[blocks, h, :, PAIR:] = bias_of(0).astype(BF16)
        v_strip[blocks, h] = jnp.zeros((BLK, PAIR), BF16)

    for copy in projection_out():
        copy.start()

    def early_group(i):
        def pick(j, b):
            c = listed[j, b]
            return jnp.where((c < 0) | (c >= blocks - LATE), blocks, c)

        picks = [[pick(j, 2 * i + n) for j in range(2)] for n in range(2)]

        def score(h):
            q = queries(i, h)
            return [dot(jnp.concatenate([k_strip[pick, h] for pick in picks[n]], axis=0), q[:, halves[n]]) for n in range(2)]

        def values(h, n):
            return jnp.concatenate([v_strip[pick, h] for pick in picks[n]], axis=1)

        def floor(h, n, top):
            return jnp.maximum(top, tops[i, h, :, halves[n]])

        def finish(h, n, part, total, top):
            weight = jnp.exp2(tops[i, h, :, halves[n]] - top)
            here = slice(h * DIM, (h + 1) * DIM)
            totals[i, h, :, halves[n]] = total + totals[i, h, :, halves[n]] * weight
            summed[i, here, halves[n]] = (tiled(part) + tiled(summed[i, here, halves[n]]) * weight).reshape(DIM, BLK)
            tops[i, h, :, halves[n]] = top

        attend(score, values, floor, finish, 2)
        for copy in sums_out(i):
            copy.start()

    def early_groups(first):
        pl.loop(first, first + 2)(early_group)

    def pass_on(c):
        x_copy(c).wait_recv()
        z_copy(c).start()

    half = groups // 2

    @pl.loop(0, groups)
    def _(j):
        pass_on(each * j)

        @pl.when(j == 0)
        def _():
            c_copy(2).wait()
            c_copy(3).start()

        @pl.when(j < half)
        def _():
            own_group(2 * j)

        @pl.when(j == groups - 1)
        def _():
            early_groups(2)

        pass_on(each * j + 1)

        @pl.when(j < half)
        def _():
            own_group(2 * j + 1)

        @pl.when(j == 0)
        def _():
            halo_group()
            c_copy(3).wait()

        @pl.when(j == groups - 1)
        def _():
            early_groups(4)

        pass_on(each * j + 2)

        @pl.when((j >= 1) & (j <= half))
        def _():
            local_group(2 * j - 2)

        @pl.when(j == groups - 1)
        def _():
            early_groups(6)

        pass_on(each * j + 3)

        @pl.when((j >= 1) & (j < half))
        def _():
            local_group(2 * j - 1)

        @pl.when(j == half)
        def _():
            local_group(groups - 1, last=True)

        @pl.when(j >= 1)
        def _():
            strip_group(j - 1)

        @pl.when(j == groups - 2)
        def _():
            early_groups(0)

    for copy in keys_out(0):
        copy.start()
    strip_group(groups - 1)

    for copy in keys_out(1):
        copy.start()

    @pl.loop(0, groups * each)
    def _(c):
        x_copy(c).wait_send()
        z_copy(c).wait_send()

    @pl.loop(0, groups)
    def _(i):
        for copy in sums_out(i) + queries_out(i):
            copy.wait()

    for copy in keys_out(0) + keys_out(1) + projection_out():
        copy.wait()


def finish_kernel(
    blocks, counts, listed, summed, tops, totals, q_hi, q_lo, k_late, v_late, w_hi, w_lo, feats, out, sums, peaks, weights
):
    i = pl.program_id(0)
    sums[...] = summed[0]
    peaks[...] = tops[0]
    weights[...] = totals[0]

    @pl.loop(0, 4)
    def _(t):
        n, j = t // 2, lax.rem(t, 2)
        pick = listed[j, 2 * i + n] - (blocks - LATE)

        @pl.when(pick >= 0)
        def _():
            columns = pl.ds(pl.multiple_of(n * BLK, BLK), BLK)

            def score(h):
                here = slice(h * DIM, (h + 1) * DIM)
                return [dot(k_late[pick, h], queries_of(q_hi[0, here, columns], q_lo[0, here, columns]))]

            def floor(h, _, top):
                return jnp.maximum(top, peaks[h, :, columns])

            def finish(h, _, part, total, top):
                weight = jnp.exp2(peaks[h, :, columns] - top)
                here = slice(h * DIM, (h + 1) * DIM)
                weights[h, :, columns] = total + weights[h, :, columns] * weight
                sums[here, columns] = (tiled(part) + tiled(sums[here, columns]) * weight).reshape(DIM, BLK)
                peaks[h, :, columns] = top

            attend(score, lambda h, _: v_late[pick, h], floor, finish, 1)

    rows = 2 * BLK
    inverse = 1.0 / weights[...]
    heads = []
    for h in range(HEADS):
        part = sums[h * DIM : (h + 1) * DIM].reshape(-1, 8, rows) * inverse[h]
        heads.append(part.reshape(DIM, rows))
    ah, al = split(jnp.concatenate(heads, axis=0).T)
    row = iota((BLK, rows), 0)
    live = jnp.concatenate([row < counts[0, 2 * i + n] for n in range(2)], axis=0)
    for p in range(feats.shape[1] // rows):
        columns = slice(p * rows, (p + 1) * rows)
        result = feats[:, columns] + dot3(ah, al, w_hi[:, columns], w_lo[:, columns])
        out[:, columns] = jnp.where(live, result, 0.0)


def body(feats, norm_gain, w_qkv, w_out, counts, partner, cross_list):
    points = feats[0]
    rows, width = points.shape
    blocks = counts.shape[1]
    groups, chunks = blocks // 2, rows // CHUNK
    hbm = pl.BlockSpec(memory_space=pl.ANY)
    vmem = pl.BlockSpec(memory_space=pltpu.VMEM)
    smem = pl.BlockSpec(memory_space=pltpu.SMEM)
    dma = pltpu.SemaphoreType.DMA
    wide = (groups, width, 2 * BLK)
    rowed = (groups, HEADS, 8, 2 * BLK)
    shapes = [
        (wide, F32), (rowed, F32), (rowed, F32), (wide, BF16), (wide, BF16),
        ((LATE + 1, HEADS, BLK, 2 * PAIR), BF16), ((LATE + 1, HEADS, PAIR, BLK), BF16),
        ((width, width), BF16), ((width, width), BF16),
    ]
    middle = pl.pallas_call(
        functools.partial(kernel, blocks),
        out_shape=[jax.ShapeDtypeStruct(*shape) for shape in shapes],
        in_specs=[hbm, vmem, hbm, hbm, smem, smem, smem],
        out_specs=[hbm] * len(shapes),
        scratch_shapes=[
            pltpu.VMEM((rows, width), F32),
            pltpu.VMEM((rows, width), F32),
            pltpu.VMEM((rows, width), F32),
            pltpu.VMEM((2 * BLK, width), F32),
            pltpu.VMEM((8, BLK), F32),
            pltpu.VMEM((4, 8, BLK), F32),
            pltpu.VMEM((4, width, width), BF16),
            pltpu.VMEM((4, width, width), BF16),
            pltpu.VMEM((groups, width, 2 * BLK), BF16),
            pltpu.VMEM((groups, width, 2 * BLK), BF16),
            pltpu.VMEM((blocks + 1, HEADS, BLK, 2 * PAIR), BF16),
            pltpu.VMEM((blocks + 1, HEADS, PAIR, BLK), BF16),
            pltpu.VMEM((blocks + 1, HEADS, BLK, 2 * PAIR), BF16),
            pltpu.VMEM((blocks + 1, HEADS, PAIR, BLK), BF16),
            pltpu.VMEM((groups, width, 2 * BLK), F32),
            pltpu.VMEM((groups, HEADS, 8, 2 * BLK), F32),
            pltpu.VMEM((groups, HEADS, 8, 2 * BLK), F32),
            dma((chunks,)), dma((chunks,)), dma((chunks,)), dma((chunks,)),
            dma((2,)), dma((2,)), dma((4,)), dma((4,)),
            dma((groups,)), dma((8,)), dma((3, groups)), dma((2, groups)), dma((2, 2)), dma((2,)),
        ],
        compiler_params=pltpu.CompilerParams(
            collective_id=0, has_side_effects=True, vmem_limit_bytes=60 * 1024 * 1024
        ),
    )(points, norm_gain.reshape(1, width), w_qkv, w_out, counts, partner, cross_list[0].T)

    def step(*shape):
        return pl.BlockSpec((1, *shape), lambda i: (i,) + (0,) * len(shape))

    def whole(*shape):
        return pl.BlockSpec(shape, lambda i: (0,) * len(shape))

    part = pl.BlockSpec((2 * BLK, width), lambda i: (i, 0))
    mixed = pl.pallas_call(
        functools.partial(finish_kernel, blocks),
        out_shape=jax.ShapeDtypeStruct((rows, width), F32),
        grid=(groups,),
        in_specs=[smem, smem]
        + [step(*shape[1:]) for shape, _ in shapes[:5]]
        + [whole(*shape) for shape, _ in shapes[5:]]
        + [part],
        out_specs=part,
        scratch_shapes=[
            pltpu.VMEM(wide[1:], F32),
            pltpu.VMEM(rowed[1:], F32),
            pltpu.VMEM(rowed[1:], F32),
        ],
        compiler_params=pltpu.CompilerParams(vmem_limit_bytes=48 * 1024 * 1024),
    )(counts, cross_list[0].T, *middle, points)
    return mixed[None]


def solution(mesh):
    in_specs = (
        P("line", "seg", None),
        P(),
        P(),
        P(),
        P("line", "seg"),
        P("line", "seg"),
        P("line", "seg", None),
    )
    out_specs = P("line", "seg", None)
    return jax.shard_map(body, mesh=mesh, in_specs=in_specs, out_specs=out_specs, check_vma=False)
```

```python
import functools
import math

import jax
import jax.numpy as jnp
from jax import lax
from jax.experimental import pallas as pl
from jax.experimental.pallas import tpu as pltpu
from jax.sharding import PartitionSpec as P

MESH = pl.DeviceIdType.MESH
F32, BF16 = jnp.float32, jnp.bfloat16
HEADS = 8
BLK = 128
DIM = 64
PAIR = 2 * DIM
CHUNK = 64
LATE = 4
BATCH = 4
PIPED = True
MASKED = -1e30
NT = (((1,), (1,)), ((), ()))


def split(x):
    high = x.astype(BF16)
    return high, (x - high.astype(F32)).astype(BF16)


def dot(a, b):
    return jnp.dot(a, b, preferred_element_type=F32)


def dot3(ah, al, bh, bl):
    return dot(ah, bh) + dot(al, bh) + dot(ah, bl)


def normalize(x, gain):
    center = x - jnp.mean(x, axis=-1, keepdims=True)
    spread = jnp.mean(center * center, axis=-1, keepdims=True)
    return center * lax.rsqrt(spread + 1e-05) * gain


def iota(shape, dim):
    return lax.broadcasted_iota(jnp.int32, shape, dim)


def dot_nt(a, b):
    return lax.dot_general(a, b, NT, preferred_element_type=F32)


def swap(x):
    return pltpu.roll(x, DIM, 1)


def tiled(x):
    return x.reshape(-1, 8, BLK)


def over_rows(reduce, x):
    return jnp.broadcast_to(reduce(reduce(tiled(x), axis=0), axis=0, keepdims=True), (8, BLK))


def attend(score, values, floor, finish, parts):
    size = 2 * BATCH // parts
    batches = [range(h, h + size) for h in range(0, HEADS, size)]
    scores = [score(h) for h in batches[0]]
    for number, batch in enumerate(batches):
        items = [(h, n) for h in batch for n in range(parts)]
        flat = [s for pair in scores for s in pair]
        if PIPED and number + 1 < len(batches):
            scores = [score(h) for h in batches[number + 1]]
        peaks = [over_rows(jnp.max, s) for s in flat]
        peaks = [floor(h, n, top) for (h, n), top in zip(items, peaks)]
        powers = [jnp.exp2(tiled(s) - top).reshape(s.shape) for s, top in zip(flat, peaks)]
        sums = [over_rows(jnp.sum, e) for e in powers]
        products = [dot(values(h, n), jnp.concatenate(split(e), axis=1)) for (h, n), e in zip(items, powers)]
        if not PIPED and number + 1 < len(batches):
            scores = [score(h) for h in batches[number + 1]]
        for (h, n), both, total, top in zip(items, products, sums, peaks):
            both = both[:, :BLK] + both[:, BLK:]
            finish(h, n, both[:DIM] + both[DIM:], total, top)


def queries_of(high, low):
    one = jnp.where(iota(high.shape, 0) == 0, 1.0, 0.0).astype(BF16)
    return jnp.concatenate([high, high, low, one], axis=0)


def kernel(
    blocks,
    feats, gain, w_qkv, w_out, counts, partner, listed,
    summed_out, tops_out, totals_out, q_hi_out, q_lo_out, k_out, v_out, w_hi_out, w_lo_out,
    own, near, far, halo, counts_row, cnt,
    w_hi, w_lo, q_hi, q_lo, k_own, v_own, k_strip, v_strip, summed, tops, totals,
    x_send, x_recv, z_send, z_recv, h_send, h_recv, c_send, c_recv,
    own_sem, w_sem, s_sem, q_sem, k_sem, p_sem,
):
    groups = blocks // 2
    rows = 2 * BLK
    each = rows // CHUNK
    width = own.shape[1]
    pairs = width // PAIR
    line, seg = lax.axis_index("line"), lax.axis_index("seg")
    lines, segs = lax.axis_size("line"), lax.axis_size("seg")
    odd = lax.rem(line, 2)
    mate = line + 1 - 2 * odd
    ahead = lax.rem(line + 2 - 4 * odd + lines, lines)
    behind = lax.rem(line - 2 + 4 * odd + lines, lines)
    right, left = lax.rem(seg + 1, segs), lax.rem(seg + segs - 1, segs)

    def group_rows(i):
        return pl.ds(pl.multiple_of(i * rows, rows), rows)

    def chunk_rows(c):
        return pl.ds(pl.multiple_of(c * CHUNK, CHUNK), CHUNK)

    def own_copy(i):
        return pltpu.make_async_copy(feats.at[group_rows(i)], own.at[group_rows(i)], own_sem.at[i])

    def w_copy(j):
        source = w_qkv.at[:, pl.ds(j * rows, rows)] if j < 6 else w_out.at[:, pl.ds((j - 6) * rows, rows)]
        return pltpu.make_async_copy(source, summed.at[j], w_sem.at[j])

    def sums_out(i):
        pairs_ = ((summed, summed_out), (tops, tops_out), (totals, totals_out))
        return [pltpu.make_async_copy(a.at[i], b.at[i], s_sem.at[n, i]) for n, (a, b) in enumerate(pairs_)]

    def queries_out(i):
        pairs_ = ((q_hi, q_hi_out), (q_lo, q_lo_out))
        return [pltpu.make_async_copy(a.at[i], b.at[i], q_sem.at[n, i]) for n, (a, b) in enumerate(pairs_)]

    def keys_out(n):
        source = pl.ds(blocks - LATE + 2 * n, 2 + n)
        target = pl.ds(2 * n, 2 + n)
        return [pltpu.make_async_copy(a.at[source], b.at[target], k_sem.at[m, n]) for m, (a, b) in enumerate(((k_strip, k_out), (v_strip, v_out)))]

    def projection_out():
        return [pltpu.make_async_copy(a.at[3], b, p_sem.at[m]) for m, (a, b) in enumerate(((w_hi, w_hi_out), (w_lo, w_lo_out)))]

    def remote(source, target, send, recv, device):
        return pltpu.make_async_remote_copy(
            src_ref=source, dst_ref=target, send_sem=send, recv_sem=recv,
            device_id=device, device_id_type=MESH,
        )

    def x_copy(c):
        return remote(feats.at[chunk_rows(c)], near.at[chunk_rows(c)], x_send.at[c], x_recv.at[c], (mate, seg))

    def z_copy(c):
        return remote(near.at[chunk_rows(c)], far.at[chunk_rows(c)], z_send.at[c], z_recv.at[c], (ahead, seg))

    def h_copy(j):
        b, device = ((blocks - 1), (line, right)) if j == 0 else (0, (line, left))
        return remote(feats.at[pl.ds(b * BLK, BLK)], halo.at[pl.ds(j * BLK, BLK)], h_send.at[j], h_recv.at[j], device)

    def c_copy(j):
        source = cnt.at[2] if j == 3 else counts_row
        device = ((line, right), (line, left), (mate, seg), (ahead, seg))[j]
        return remote(source, cnt.at[j], c_send.at[j], c_recv.at[j], device)

    barrier = pltpu.get_barrier_semaphore()
    for device in ((mate, seg), (ahead, seg), (behind, seg), (line, right), (line, left)):
        pl.semaphore_signal(barrier, inc=1, device_id=device, device_id_type=MESH)
    for i in range(groups):
        own_copy(i).start()
    for j in range(8):
        w_copy(j).start()
    lane = iota((8, BLK), 1)
    filled = jnp.zeros((8, BLK), F32)
    for b in range(blocks):
        filled = jnp.where(lane == b, counts[0, b].astype(F32), filled)
    counts_row[...] = filled
    pl.semaphore_wait(barrier, 5)
    for j in range(3):
        c_copy(j).start()
    for j in range(2):
        h_copy(j).start()

    @pl.loop(0, groups * each)
    def _(c):
        x_copy(c).start()

    for j in range(8):
        w_copy(j).wait()
        w = summed[j]
        if j < 2:
            w = w * (DIM**-0.5 * math.log2(math.e))
        if j // 2 in (0, 2):
            w = w.T
            where = (pl.ds(j % 2 * rows, rows), slice(None))
        else:
            where = (slice(None), pl.ds(j % 2 * rows, rows))
        high, rest = split(w)
        w_hi[(j // 2, *where)] = high
        w_lo[(j // 2, *where)] = rest

    def low(n):
        return iota((n, PAIR), 1) < DIM

    def mark(n):
        return iota((n, PAIR), 1) == DIM

    def weights(j, p):
        columns = pl.ds(p * rows, rows)
        return w_hi[j, :, columns], w_lo[j, :, columns]

    def project_across(j, xh, xl):
        wh, wl = w_hi[j], w_lo[j]
        return split(dot_nt(wh, xh) + dot_nt(wh, xl) + dot_nt(wl, xh))

    def bias_of(count):
        dead = (iota((BLK, PAIR), 0) >= count) & mark(BLK)
        return jnp.where(dead, MASKED, 0.0)

    def count_in(row, b):
        return jnp.sum(jnp.where(iota(row.shape, 1) == b, row, 0.0), axis=1, keepdims=True).astype(jnp.int32)

    def store_keys(xh, xl, k_ref, v_ref, slots, bias):
        lo = low(rows)
        for p in range(pairs // 2):
            both = dot3(xh, xl, *weights(1, p))
            for half in range(2):
                h = 4 * p + 2 * half
                k = both[:, half * PAIR : (half + 1) * PAIR]
                kh = k.astype(BF16).astype(F32)
                kl = k - kh
                kh_, kl_ = swap(kh), swap(kl)
                for head, a, b in ((h, jnp.where(lo, kh, kl_), kh), (h + 1, jnp.where(lo, kh_, kl), kh_)):
                    a = a.astype(BF16)
                    b = jnp.where(lo, b, bias).astype(BF16)
                    for n, slot in enumerate(slots):
                        k_ref[slot, head, :, :PAIR] = a[n * BLK : (n + 1) * BLK]
                        k_ref[slot, head, :, PAIR:] = b[n * BLK : (n + 1) * BLK]
        vh, vl = project_across(2, xh, xl)
        for h in range(HEADS):
            for n, slot in enumerate(slots):
                part = (slice(h * DIM, (h + 1) * DIM), slice(n * BLK, (n + 1) * BLK))
                v_ref[slot, h, :DIM] = vh[part]
                v_ref[slot, h, DIM:] = vl[part]

    def own_group(i):
        own_copy(i).wait()
        xh, xl = split(normalize(own[group_rows(i)], gain[...]))
        q_hi[i], q_lo[i] = project_across(0, xh, xl)
        for copy in queries_out(i):
            copy.start()
        bias = jnp.concatenate([bias_of(counts[0, 2 * i]), bias_of(counts[0, 2 * i + 1])], axis=0)
        store_keys(xh, xl, k_own, v_own, (2 * i, 2 * i + 1), bias)

    def halo_group():
        for j in range(2):
            h_copy(j).wait()
            c_copy(j).wait()
        xh, xl = split(normalize(halo[...], gain[...]))
        before = jnp.where(seg == 0, 0, count_in(cnt[0, 0:1], blocks - 1))
        after = jnp.where(seg == segs - 1, 0, count_in(cnt[1, 0:1], 0))
        bias = jnp.concatenate([bias_of(before), bias_of(after)], axis=0)
        store_keys(xh, xl, k_own, v_own, (blocks - 1, blocks), bias)

    use_near = lax.rem(partner[0, 0] + odd, 2) == 1

    def strip_group(i):
        for n in range(each):
            z_copy(each * i + n).wait_recv()
        x = jnp.where(use_near, near[group_rows(i)], far[group_rows(i)])
        row = jnp.where(use_near, cnt[2, 0:1], cnt[3, 0:1])
        xh, xl = split(normalize(x, gain[...]))
        bias = jnp.concatenate([bias_of(count_in(row, 2 * i)), bias_of(count_in(row, 2 * i + 1))], axis=0)
        store_keys(xh, xl, k_strip, v_strip, (2 * i, 2 * i + 1), bias)

    def queries(i, h):
        part = slice(h * DIM, (h + 1) * DIM)
        return queries_of(q_hi[i, part], q_lo[i, part])

    halves = [slice(n * BLK, (n + 1) * BLK) for n in range(2)]

    def local_group(i, last=False):
        slots = [lax.rem(2 * i - 1 + j + blocks, blocks) for j in range(4)]
        if last:
            slots[3] = blocks

        def score(h):
            k = jnp.concatenate([k_own[slot, h] for slot in slots], axis=0)
            s = dot(k, queries(i, h))
            return [s[n * BLK : (n + 3) * BLK, halves[n]] for n in range(2)]

        def values(h, n):
            return jnp.concatenate([v_own[slot, h] for slot in slots[n : n + 3]], axis=1)

        def finish(h, n, part, total, top):
            summed[i, h * DIM : (h + 1) * DIM, halves[n]] = part
            tops[i, h, :, halves[n]] = top
            totals[i, h, :, halves[n]] = total

        attend(score, values, lambda h, n, top: top, finish, 2)

    for h in range(HEADS):
        k_strip[blocks, h, :, :PAIR] = jnp.zeros((BLK, PAIR), BF16)
        k_strip[blocks, h, :, PAIR:] = bias_of(0).astype(BF16)
        v_strip[blocks, h] = jnp.zeros((BLK, PAIR), BF16)

    for copy in projection_out():
        copy.start()

    def early_group(i):
        def pick(j, b):
            c = listed[j, b]
            return jnp.where((c < 0) | (c >= blocks - LATE), blocks, c)

        picks = [[pick(j, 2 * i + n) for j in range(2)] for n in range(2)]

        def score(h):
            q = queries(i, h)
            return [dot(jnp.concatenate([k_strip[pick, h] for pick in picks[n]], axis=0), q[:, halves[n]]) for n in range(2)]

        def values(h, n):
            return jnp.concatenate([v_strip[pick, h] for pick in picks[n]], axis=1)

        def floor(h, n, top):
            return jnp.maximum(top, tops[i, h, :, halves[n]])

        def finish(h, n, part, total, top):
            weight = jnp.exp2(tops[i, h, :, halves[n]] - top)
            here = slice(h * DIM, (h + 1) * DIM)
            totals[i, h, :, halves[n]] = total + totals[i, h, :, halves[n]] * weight
            summed[i, here, halves[n]] = (tiled(part) + tiled(summed[i, here, halves[n]]) * weight).reshape(DIM, BLK)
            tops[i, h, :, halves[n]] = top

        attend(score, values, floor, finish, 2)
        for copy in sums_out(i):
            copy.start()

    def early_groups(first):
        pl.loop(first, first + 2)(early_group)

    def pass_on(c):
        x_copy(c).wait_recv()
        z_copy(c).start()

    half = groups // 2

    @pl.loop(0, groups)
    def _(j):
        pass_on(each * j)

        @pl.when(j == 0)
        def _():
            c_copy(2).wait()
            c_copy(3).start()

        @pl.when(j < half)
        def _():
            own_group(2 * j)

        @pl.when(j == groups - 1)
        def _():
            early_groups(2)

        pass_on(each * j + 1)

        @pl.when(j < half)
        def _():
            own_group(2 * j + 1)

        @pl.when(j == 0)
        def _():
            halo_group()
            c_copy(3).wait()

        @pl.when(j == groups - 1)
        def _():
            early_groups(4)

        pass_on(each * j + 2)

        @pl.when((j >= 1) & (j <= half))
        def _():
            local_group(2 * j - 2)

        @pl.when(j == groups - 1)
        def _():
            early_groups(6)

        pass_on(each * j + 3)

        @pl.when((j >= 1) & (j < half))
        def _():
            local_group(2 * j - 1)

        @pl.when(j == half)
        def _():
            local_group(groups - 1, last=True)

        @pl.when(j >= 1)
        def _():
            strip_group(j - 1)

        @pl.when(j == groups - 2)
        def _():
            early_groups(0)

    for copy in keys_out(0):
        copy.start()
    strip_group(groups - 1)

    for copy in keys_out(1):
        copy.start()

    @pl.loop(0, groups * each)
    def _(c):
        x_copy(c).wait_send()
        z_copy(c).wait_send()

    @pl.loop(0, groups)
    def _(i):
        for copy in sums_out(i) + queries_out(i):
            copy.wait()

    for copy in keys_out(0) + keys_out(1) + projection_out():
        copy.wait()


def finish_kernel(
    blocks, counts, listed, summed_in, tops_in, totals_in, q_hi_in, q_lo_in, k_in, v_in, w_hi_in, w_lo_in, feats, out,
    summed, tops, totals, q_hi, q_lo, k_late, v_late, w_hi, w_lo, rest, g_sem, a_sem, out_sem,
):
    groups = blocks // 2
    rows = 2 * BLK

    def group_rows(i):
        return pl.ds(pl.multiple_of(i * rows, rows), rows)

    def group_copies(i):
        refs = ((summed_in.at[i], summed.at[i]), (q_hi_in.at[i], q_hi.at[i]), (q_lo_in.at[i], q_lo.at[i]), (feats.at[group_rows(i)], rest.at[group_rows(i)]))
        return [pltpu.make_async_copy(*pair, g_sem.at[n, i]) for n, pair in enumerate(refs)]

    refs = ((k_in, k_late), (v_in, v_late), (tops_in, tops), (totals_in, totals), (w_hi_in, w_hi), (w_lo_in, w_lo))
    shared = [pltpu.make_async_copy(*pair, a_sem.at[n]) for n, pair in enumerate(refs)]

    def out_copy(i):
        return pltpu.make_async_copy(rest.at[group_rows(i)], out.at[group_rows(i)], out_sem.at[i])

    for copy in shared:
        copy.start()

    @pl.loop(0, groups)
    def _(i):
        for copy in group_copies(i):
            copy.start()

    for copy in shared:
        copy.wait()

    @pl.loop(0, groups)
    def _(i):
        for copy in group_copies(i):
            copy.wait()

        @pl.loop(0, 4)
        def _(t):
            n, j = t // 2, lax.rem(t, 2)
            pick = listed[j, 2 * i + n] - (blocks - LATE)

            @pl.when(pick >= 0)
            def _():
                columns = pl.ds(pl.multiple_of(n * BLK, BLK), BLK)

                def score(h):
                    here = slice(h * DIM, (h + 1) * DIM)
                    return [dot(k_late[pick, h], queries_of(q_hi[i, here, columns], q_lo[i, here, columns]))]

                def floor(h, _, top):
                    return jnp.maximum(top, tops[i, h, :, columns])

                def finish(h, _, part, total, top):
                    weight = jnp.exp2(tops[i, h, :, columns] - top)
                    here = slice(h * DIM, (h + 1) * DIM)
                    totals[i, h, :, columns] = total + totals[i, h, :, columns] * weight
                    summed[i, here, columns] = (tiled(part) + tiled(summed[i, here, columns]) * weight).reshape(DIM, BLK)
                    tops[i, h, :, columns] = top

                attend(score, lambda h, _: v_late[pick, h], floor, finish, 1)

        inverse = 1.0 / totals[i]
        heads = []
        for h in range(HEADS):
            part = summed[i, h * DIM : (h + 1) * DIM].reshape(-1, 8, rows) * inverse[h]
            heads.append(part.reshape(DIM, rows))
        ah, al = split(jnp.concatenate(heads, axis=0).T)
        row = iota((BLK, rows), 0)
        live = jnp.concatenate([row < counts[0, 2 * i + n] for n in range(2)], axis=0)
        r = group_rows(i)
        for p in range(rest.shape[1] // rows):
            columns = slice(p * rows, (p + 1) * rows)
            result = rest[r, columns] + dot3(ah, al, w_hi[:, columns], w_lo[:, columns])
            rest[r, columns] = jnp.where(live, result, 0.0)
        out_copy(i).start()

    for i in range(groups):
        out_copy(i).wait()


def body(feats, norm_gain, w_qkv, w_out, counts, partner, cross_list):
    points = feats[0]
    rows, width = points.shape
    blocks = counts.shape[1]
    groups, chunks = blocks // 2, rows // CHUNK
    hbm = pl.BlockSpec(memory_space=pl.ANY)
    vmem = pl.BlockSpec(memory_space=pltpu.VMEM)
    smem = pl.BlockSpec(memory_space=pltpu.SMEM)
    dma = pltpu.SemaphoreType.DMA
    wide = (groups, width, 2 * BLK)
    rowed = (groups, HEADS, 8, 2 * BLK)
    shapes = [
        (wide, F32), (rowed, F32), (rowed, F32), (wide, BF16), (wide, BF16),
        ((LATE + 1, HEADS, BLK, 2 * PAIR), BF16), ((LATE + 1, HEADS, PAIR, BLK), BF16),
        ((width, width), BF16), ((width, width), BF16),
    ]
    middle = pl.pallas_call(
        functools.partial(kernel, blocks),
        out_shape=[jax.ShapeDtypeStruct(*shape) for shape in shapes],
        in_specs=[hbm, vmem, hbm, hbm, smem, smem, smem],
        out_specs=[hbm] * len(shapes),
        scratch_shapes=[
            pltpu.VMEM((rows, width), F32),
            pltpu.VMEM((rows, width), F32),
            pltpu.VMEM((rows, width), F32),
            pltpu.VMEM((2 * BLK, width), F32),
            pltpu.VMEM((8, BLK), F32),
            pltpu.VMEM((4, 8, BLK), F32),
            pltpu.VMEM((4, width, width), BF16),
            pltpu.VMEM((4, width, width), BF16),
            pltpu.VMEM((groups, width, 2 * BLK), BF16),
            pltpu.VMEM((groups, width, 2 * BLK), BF16),
            pltpu.VMEM((blocks + 1, HEADS, BLK, 2 * PAIR), BF16),
            pltpu.VMEM((blocks + 1, HEADS, PAIR, BLK), BF16),
            pltpu.VMEM((blocks + 1, HEADS, BLK, 2 * PAIR), BF16),
            pltpu.VMEM((blocks + 1, HEADS, PAIR, BLK), BF16),
            pltpu.VMEM((groups, width, 2 * BLK), F32),
            pltpu.VMEM((groups, HEADS, 8, 2 * BLK), F32),
            pltpu.VMEM((groups, HEADS, 8, 2 * BLK), F32),
            dma((chunks,)), dma((chunks,)), dma((chunks,)), dma((chunks,)),
            dma((2,)), dma((2,)), dma((4,)), dma((4,)),
            dma((groups,)), dma((8,)), dma((3, groups)), dma((2, groups)), dma((2, 2)), dma((2,)),
        ],
        compiler_params=pltpu.CompilerParams(
            collective_id=0, has_side_effects=True, vmem_limit_bytes=60 * 1024 * 1024
        ),
    )(points, norm_gain.reshape(1, width), w_qkv, w_out, counts, partner, cross_list[0].T)

    mixed = pl.pallas_call(
        functools.partial(finish_kernel, blocks),
        out_shape=jax.ShapeDtypeStruct((rows, width), F32),
        in_specs=[smem, smem] + [hbm] * (len(shapes) + 1),
        out_specs=hbm,
        scratch_shapes=[pltpu.VMEM(*shape) for shape in shapes]
        + [pltpu.VMEM((rows, width), F32), dma((4, groups)), dma((6,)), dma((groups,))],
        compiler_params=pltpu.CompilerParams(vmem_limit_bytes=60 * 1024 * 1024),
    )(counts, cross_list[0].T, *middle, points)
    return mixed[None]


def solution(mesh):
    in_specs = (
        P("line", "seg", None),
        P(),
        P(),
        P(),
        P("line", "seg"),
        P("line", "seg"),
        P("line", "seg", None),
    )
    out_specs = P("line", "seg", None)
    return jax.shard_map(body, mesh=mesh, in_specs=in_specs, out_specs=out_specs, check_vma=False)
```

```python
import functools
import math

import jax
import jax.numpy as jnp
from jax import lax
from jax.experimental import pallas as pl
from jax.experimental.pallas import tpu as pltpu
from jax.sharding import PartitionSpec as P

MESH = pl.DeviceIdType.MESH
F32, BF16 = jnp.float32, jnp.bfloat16
HEADS = 8
BLK = 128
DIM = 64
PAIR = 2 * DIM
CHUNK = 64
LATE = 4
BATCH = 4
PIPED = True
MASKED = -1e30
NT = (((1,), (1,)), ((), ()))


def split(x):
    high = x.astype(BF16)
    return high, (x - high.astype(F32)).astype(BF16)


def dot(a, b):
    return jnp.dot(a, b, preferred_element_type=F32)


def dot3(ah, al, bh, bl):
    return dot(ah, bh) + dot(al, bh) + dot(ah, bl)


def normalize(x, gain):
    center = x - jnp.mean(x, axis=-1, keepdims=True)
    spread = jnp.mean(center * center, axis=-1, keepdims=True)
    return center * lax.rsqrt(spread + 1e-05) * gain


def iota(shape, dim):
    return lax.broadcasted_iota(jnp.int32, shape, dim)


def dot_nt(a, b):
    return lax.dot_general(a, b, NT, preferred_element_type=F32)


def swap(x):
    return pltpu.roll(x, DIM, 1)


def tiled(x):
    return x.reshape(-1, 8, BLK)


def over_rows(reduce, x):
    return jnp.broadcast_to(reduce(reduce(tiled(x), axis=0), axis=0, keepdims=True), (8, BLK))


def attend(score, values, floor, finish, parts):
    size = 2 * BATCH // parts
    batches = [range(h, h + size) for h in range(0, HEADS, size)]
    scores = [score(h) for h in batches[0]]
    for number, batch in enumerate(batches):
        items = [(h, n) for h in batch for n in range(parts)]
        flat = [s for pair in scores for s in pair]
        if PIPED and number + 1 < len(batches):
            scores = [score(h) for h in batches[number + 1]]
        peaks = [over_rows(jnp.max, s) for s in flat]
        peaks = [floor(h, n, top) for (h, n), top in zip(items, peaks)]
        powers = [jnp.exp2(tiled(s) - top).reshape(s.shape) for s, top in zip(flat, peaks)]
        sums = [over_rows(jnp.sum, e) for e in powers]
        products = [dot(values(h, n), jnp.concatenate(split(e), axis=1)) for (h, n), e in zip(items, powers)]
        if not PIPED and number + 1 < len(batches):
            scores = [score(h) for h in batches[number + 1]]
        for (h, n), both, total, top in zip(items, products, sums, peaks):
            both = both[:, :BLK] + both[:, BLK:]
            finish(h, n, both[:DIM] + both[DIM:], total, top)


def queries_of(high, low):
    one = jnp.where(iota(high.shape, 0) == 0, 1.0, 0.0).astype(BF16)
    return jnp.concatenate([high, high, low, one], axis=0)


def kernel(
    blocks,
    feats, gain, w_qkv, w_out, counts, partner, listed,
    summed_out, tops_out, totals_out, q_hi_out, q_lo_out, k_out, m_out, v_out, w_hi_out, w_lo_out,
    own, near, far, halo, counts_row, cnt,
    w_hi, w_lo, q_hi, q_lo, k_own, v_own, k_strip, v_strip, summed, tops, totals,
    x_send, x_recv, z_send, z_recv, h_send, h_recv, c_send, c_recv,
    own_sem, w_sem, s_sem, q_sem, k_sem, p_sem,
):
    groups = blocks // 2
    rows = 2 * BLK
    each = rows // CHUNK
    width = own.shape[1]
    pairs = width // PAIR
    line, seg = lax.axis_index("line"), lax.axis_index("seg")
    lines, segs = lax.axis_size("line"), lax.axis_size("seg")
    odd = lax.rem(line, 2)
    mate = line + 1 - 2 * odd
    ahead = lax.rem(line + 2 - 4 * odd + lines, lines)
    behind = lax.rem(line - 2 + 4 * odd + lines, lines)
    right, left = lax.rem(seg + 1, segs), lax.rem(seg + segs - 1, segs)

    def group_rows(i):
        return pl.ds(pl.multiple_of(i * rows, rows), rows)

    def chunk_rows(c):
        return pl.ds(pl.multiple_of(c * CHUNK, CHUNK), CHUNK)

    def own_copy(i):
        return pltpu.make_async_copy(feats.at[group_rows(i)], own.at[group_rows(i)], own_sem.at[i])

    def w_copy(j):
        source = w_qkv.at[:, pl.ds(j * rows, rows)] if j < 6 else w_out.at[:, pl.ds((j - 6) * rows, rows)]
        return pltpu.make_async_copy(source, summed.at[j], w_sem.at[j])

    def sums_out(i):
        pairs_ = ((summed, summed_out), (tops, tops_out), (totals, totals_out))
        return [pltpu.make_async_copy(a.at[i], b.at[i], s_sem.at[n, i]) for n, (a, b) in enumerate(pairs_)]

    def queries_out(i):
        pairs_ = ((q_hi, q_hi_out), (q_lo, q_lo_out))
        return [pltpu.make_async_copy(a.at[i], b.at[i], q_sem.at[n, i]) for n, (a, b) in enumerate(pairs_)]

    def keys_out(n):
        source = pl.ds(blocks - LATE + 2 * n, 2 + n)
        target = pl.ds(2 * n, 2 + n)
        pairs_ = (
            (k_strip.at[source, :, :, pl.ds(0, PAIR)], k_out),
            (k_strip.at[source, 0, :, pl.ds(PAIR, PAIR)], m_out),
            (v_strip.at[source], v_out),
        )
        return [pltpu.make_async_copy(a, b.at[target], k_sem.at[m, n]) for m, (a, b) in enumerate(pairs_)]

    def projection_out():
        return [pltpu.make_async_copy(a.at[3], b, p_sem.at[m]) for m, (a, b) in enumerate(((w_hi, w_hi_out), (w_lo, w_lo_out)))]

    def remote(source, target, send, recv, device):
        return pltpu.make_async_remote_copy(
            src_ref=source, dst_ref=target, send_sem=send, recv_sem=recv,
            device_id=device, device_id_type=MESH,
        )

    def x_copy(c):
        return remote(feats.at[chunk_rows(c)], near.at[chunk_rows(c)], x_send.at[c], x_recv.at[c], (mate, seg))

    def z_copy(c):
        return remote(near.at[chunk_rows(c)], far.at[chunk_rows(c)], z_send.at[c], z_recv.at[c], (ahead, seg))

    def h_copy(j):
        b, device = ((blocks - 1), (line, right)) if j == 0 else (0, (line, left))
        return remote(feats.at[pl.ds(b * BLK, BLK)], halo.at[pl.ds(j * BLK, BLK)], h_send.at[j], h_recv.at[j], device)

    def c_copy(j):
        source = cnt.at[2] if j == 3 else counts_row
        device = ((line, right), (line, left), (mate, seg), (ahead, seg))[j]
        return remote(source, cnt.at[j], c_send.at[j], c_recv.at[j], device)

    barrier = pltpu.get_barrier_semaphore()
    for device in ((mate, seg), (ahead, seg), (behind, seg), (line, right), (line, left)):
        pl.semaphore_signal(barrier, inc=1, device_id=device, device_id_type=MESH)
    for i in range(groups):
        own_copy(i).start()
    for j in range(8):
        w_copy(j).start()
    lane = iota((8, BLK), 1)
    filled = jnp.zeros((8, BLK), F32)
    for b in range(blocks):
        filled = jnp.where(lane == b, counts[0, b].astype(F32), filled)
    counts_row[...] = filled
    pl.semaphore_wait(barrier, 5)
    for j in range(3):
        c_copy(j).start()
    for j in range(2):
        h_copy(j).start()

    @pl.loop(0, groups * each)
    def _(c):
        x_copy(c).start()

    for j in range(8):
        w_copy(j).wait()
        w = summed[j]
        if j < 2:
            w = w * (DIM**-0.5 * math.log2(math.e))
        if j // 2 in (0, 2):
            w = w.T
            where = (pl.ds(j % 2 * rows, rows), slice(None))
        else:
            where = (slice(None), pl.ds(j % 2 * rows, rows))
        high, rest = split(w)
        w_hi[(j // 2, *where)] = high
        w_lo[(j // 2, *where)] = rest

    def low(n):
        return iota((n, PAIR), 1) < DIM

    def mark(n):
        return iota((n, PAIR), 1) == DIM

    def weights(j, p):
        columns = pl.ds(p * rows, rows)
        return w_hi[j, :, columns], w_lo[j, :, columns]

    def project_across(j, xh, xl):
        wh, wl = w_hi[j], w_lo[j]
        return split(dot_nt(wh, xh) + dot_nt(wh, xl) + dot_nt(wl, xh))

    def bias_of(count):
        dead = (iota((BLK, PAIR), 0) >= count) & mark(BLK)
        return jnp.where(dead, MASKED, 0.0)

    def count_in(row, b):
        return jnp.sum(jnp.where(iota(row.shape, 1) == b, row, 0.0), axis=1, keepdims=True).astype(jnp.int32)

    def store_keys(xh, xl, k_ref, v_ref, slots, bias):
        lo = low(rows)
        for p in range(pairs // 2):
            both = dot3(xh, xl, *weights(1, p))
            for half in range(2):
                h = 4 * p + 2 * half
                k = both[:, half * PAIR : (half + 1) * PAIR]
                kh = k.astype(BF16).astype(F32)
                kl = k - kh
                kh_, kl_ = swap(kh), swap(kl)
                for head, a, b in ((h, jnp.where(lo, kh, kl_), kh), (h + 1, jnp.where(lo, kh_, kl), kh_)):
                    a = a.astype(BF16)
                    b = jnp.where(lo, b, bias).astype(BF16)
                    for n, slot in enumerate(slots):
                        k_ref[slot, head, :, :PAIR] = a[n * BLK : (n + 1) * BLK]
                        k_ref[slot, head, :, PAIR:] = b[n * BLK : (n + 1) * BLK]
        vh, vl = project_across(2, xh, xl)
        for h in range(HEADS):
            for n, slot in enumerate(slots):
                part = (slice(h * DIM, (h + 1) * DIM), slice(n * BLK, (n + 1) * BLK))
                v_ref[slot, h, :DIM] = vh[part]
                v_ref[slot, h, DIM:] = vl[part]

    def own_group(i):
        own_copy(i).wait()
        xh, xl = split(normalize(own[group_rows(i)], gain[...]))
        q_hi[i], q_lo[i] = project_across(0, xh, xl)
        for copy in queries_out(i):
            copy.start()
        bias = jnp.concatenate([bias_of(counts[0, 2 * i]), bias_of(counts[0, 2 * i + 1])], axis=0)
        store_keys(xh, xl, k_own, v_own, (2 * i, 2 * i + 1), bias)

    def halo_group():
        for j in range(2):
            h_copy(j).wait()
            c_copy(j).wait()
        xh, xl = split(normalize(halo[...], gain[...]))
        before = jnp.where(seg == 0, 0, count_in(cnt[0, 0:1], blocks - 1))
        after = jnp.where(seg == segs - 1, 0, count_in(cnt[1, 0:1], 0))
        bias = jnp.concatenate([bias_of(before), bias_of(after)], axis=0)
        store_keys(xh, xl, k_own, v_own, (blocks - 1, blocks), bias)

    use_near = lax.rem(partner[0, 0] + odd, 2) == 1

    def strip_group(i):
        for n in range(each):
            z_copy(each * i + n).wait_recv()
        x = jnp.where(use_near, near[group_rows(i)], far[group_rows(i)])
        row = jnp.where(use_near, cnt[2, 0:1], cnt[3, 0:1])
        xh, xl = split(normalize(x, gain[...]))
        bias = jnp.concatenate([bias_of(count_in(row, 2 * i)), bias_of(count_in(row, 2 * i + 1))], axis=0)
        store_keys(xh, xl, k_strip, v_strip, (2 * i, 2 * i + 1), bias)

    def queries(i, h):
        part = slice(h * DIM, (h + 1) * DIM)
        return queries_of(q_hi[i, part], q_lo[i, part])

    halves = [slice(n * BLK, (n + 1) * BLK) for n in range(2)]

    def local_group(i, last=False):
        slots = [lax.rem(2 * i - 1 + j + blocks, blocks) for j in range(4)]
        if last:
            slots[3] = blocks

        def score(h):
            k = jnp.concatenate([k_own[slot, h] for slot in slots], axis=0)
            s = dot(k, queries(i, h))
            return [s[n * BLK : (n + 3) * BLK, halves[n]] for n in range(2)]

        def values(h, n):
            return jnp.concatenate([v_own[slot, h] for slot in slots[n : n + 3]], axis=1)

        def finish(h, n, part, total, top):
            summed[i, h * DIM : (h + 1) * DIM, halves[n]] = part
            tops[i, h, :, halves[n]] = top
            totals[i, h, :, halves[n]] = total

        attend(score, values, lambda h, n, top: top, finish, 2)

    for h in range(HEADS):
        k_strip[blocks, h, :, :PAIR] = jnp.zeros((BLK, PAIR), BF16)
        k_strip[blocks, h, :, PAIR:] = bias_of(0).astype(BF16)
        v_strip[blocks, h] = jnp.zeros((BLK, PAIR), BF16)

    for copy in projection_out():
        copy.start()

    def early_group(i):
        def pick(j, b):
            c = listed[j, b]
            return jnp.where((c < 0) | (c >= blocks - LATE), blocks, c)

        picks = [[pick(j, 2 * i + n) for j in range(2)] for n in range(2)]

        def score(h):
            q = queries(i, h)
            return [dot(jnp.concatenate([k_strip[pick, h] for pick in picks[n]], axis=0), q[:, halves[n]]) for n in range(2)]

        def values(h, n):
            return jnp.concatenate([v_strip[pick, h] for pick in picks[n]], axis=1)

        def floor(h, n, top):
            return jnp.maximum(top, tops[i, h, :, halves[n]])

        def finish(h, n, part, total, top):
            weight = jnp.exp2(tops[i, h, :, halves[n]] - top)
            here = slice(h * DIM, (h + 1) * DIM)
            totals[i, h, :, halves[n]] = total + totals[i, h, :, halves[n]] * weight
            summed[i, here, halves[n]] = (tiled(part) + tiled(summed[i, here, halves[n]]) * weight).reshape(DIM, BLK)
            tops[i, h, :, halves[n]] = top

        attend(score, values, floor, finish, 2)
        for copy in sums_out(i):
            copy.start()

    def early_groups(first):
        pl.loop(first, first + 2)(early_group)

    def pass_on(c):
        x_copy(c).wait_recv()
        z_copy(c).start()

    half = groups // 2

    @pl.loop(0, groups)
    def _(j):
        pass_on(each * j)

        @pl.when(j == 0)
        def _():
            c_copy(2).wait()
            c_copy(3).start()

        @pl.when(j < half)
        def _():
            own_group(2 * j)

        @pl.when(j == groups - 1)
        def _():
            early_groups(2)

        pass_on(each * j + 1)

        @pl.when(j < half)
        def _():
            own_group(2 * j + 1)

        @pl.when(j == 0)
        def _():
            halo_group()
            c_copy(3).wait()

        @pl.when(j == groups - 1)
        def _():
            early_groups(4)

        pass_on(each * j + 2)

        @pl.when((j >= 1) & (j <= half))
        def _():
            local_group(2 * j - 2)

        @pl.when(j == groups - 1)
        def _():
            early_groups(6)

        pass_on(each * j + 3)

        @pl.when((j >= 1) & (j < half))
        def _():
            local_group(2 * j - 1)

        @pl.when(j == half)
        def _():
            local_group(groups - 1, last=True)

        @pl.when(j >= 1)
        def _():
            strip_group(j - 1)

        @pl.when(j == groups - 2)
        def _():
            early_groups(0)

    for copy in keys_out(0):
        copy.start()
    strip_group(groups - 1)

    for copy in keys_out(1):
        copy.start()

    @pl.loop(0, groups * each)
    def _(c):
        x_copy(c).wait_send()
        z_copy(c).wait_send()

    @pl.loop(0, groups)
    def _(i):
        for copy in sums_out(i) + queries_out(i):
            copy.wait()

    for copy in keys_out(0) + keys_out(1) + projection_out():
        copy.wait()


def finish_kernel(
    blocks, counts, listed, summed_in, tops_in, totals_in, q_hi_in, q_lo_in, k_in, m_in, v_in, w_hi_in, w_lo_in, feats, out,
    summed, tops, totals, q_hi, q_lo, k_late, m_late, v_late, w_hi, w_lo, rest, g_sem, a_sem, out_sem,
):
    groups = blocks // 2
    rows = 2 * BLK

    def group_rows(i):
        return pl.ds(pl.multiple_of(i * rows, rows), rows)

    def group_copies(i):
        refs = ((summed_in.at[i], summed.at[i]), (q_hi_in.at[i], q_hi.at[i]), (q_lo_in.at[i], q_lo.at[i]), (feats.at[group_rows(i)], rest.at[group_rows(i)]))
        return [pltpu.make_async_copy(*pair, g_sem.at[n, i]) for n, pair in enumerate(refs)]

    refs = ((k_in, k_late), (m_in, m_late), (v_in, v_late), (tops_in, tops), (totals_in, totals), (w_hi_in, w_hi), (w_lo_in, w_lo))
    shared = [pltpu.make_async_copy(*pair, a_sem.at[n]) for n, pair in enumerate(refs)]

    def out_copy(i):
        return pltpu.make_async_copy(rest.at[group_rows(i)], out.at[group_rows(i)], out_sem.at[i])

    for copy in group_copies(0) + shared:
        copy.start()

    @pl.loop(1, groups)
    def _(i):
        for copy in group_copies(i):
            copy.start()

    for copy in shared:
        copy.wait()

    @pl.loop(0, groups)
    def _(i):
        for copy in group_copies(i):
            copy.wait()

        @pl.loop(0, 4)
        def _(t):
            n, j = t // 2, lax.rem(t, 2)
            pick = listed[j, 2 * i + n] - (blocks - LATE)

            @pl.when(pick >= 0)
            def _():
                columns = pl.ds(pl.multiple_of(n * BLK, BLK), BLK)
                lo = iota((BLK, PAIR), 1) < DIM
                masks = m_late[pick].astype(F32)

                def score(h):
                    here = slice(h * DIM, (h + 1) * DIM)
                    k = k_late[pick, h]
                    again = jnp.where(lo, k.astype(F32), masks).astype(BF16)
                    return [dot(jnp.concatenate([k, again], axis=1), queries_of(q_hi[i, here, columns], q_lo[i, here, columns]))]

                def floor(h, _, top):
                    return jnp.maximum(top, tops[i, h, :, columns])

                def finish(h, _, part, total, top):
                    weight = jnp.exp2(tops[i, h, :, columns] - top)
                    here = slice(h * DIM, (h + 1) * DIM)
                    totals[i, h, :, columns] = total + totals[i, h, :, columns] * weight
                    summed[i, here, columns] = (tiled(part) + tiled(summed[i, here, columns]) * weight).reshape(DIM, BLK)
                    tops[i, h, :, columns] = top

                attend(score, lambda h, _: v_late[pick, h], floor, finish, 1)

        inverse = 1.0 / totals[i]
        heads = []
        for h in range(HEADS):
            part = summed[i, h * DIM : (h + 1) * DIM].reshape(-1, 8, rows) * inverse[h]
            heads.append(part.reshape(DIM, rows))
        ah, al = split(jnp.concatenate(heads, axis=0).T)
        row = iota((BLK, rows), 0)
        live = jnp.concatenate([row < counts[0, 2 * i + n] for n in range(2)], axis=0)
        r = group_rows(i)
        for p in range(rest.shape[1] // rows):
            columns = slice(p * rows, (p + 1) * rows)
            result = rest[r, columns] + dot3(ah, al, w_hi[:, columns], w_lo[:, columns])
            rest[r, columns] = jnp.where(live, result, 0.0)
        out_copy(i).start()

    for i in range(groups):
        out_copy(i).wait()


def body(feats, norm_gain, w_qkv, w_out, counts, partner, cross_list):
    points = feats[0]
    rows, width = points.shape
    blocks = counts.shape[1]
    groups, chunks = blocks // 2, rows // CHUNK
    hbm = pl.BlockSpec(memory_space=pl.ANY)
    vmem = pl.BlockSpec(memory_space=pltpu.VMEM)
    smem = pl.BlockSpec(memory_space=pltpu.SMEM)
    dma = pltpu.SemaphoreType.DMA
    wide = (groups, width, 2 * BLK)
    rowed = (groups, HEADS, 8, 2 * BLK)
    shapes = [
        (wide, F32), (rowed, F32), (rowed, F32), (wide, BF16), (wide, BF16),
        ((LATE + 1, HEADS, BLK, PAIR), BF16), ((LATE + 1, BLK, PAIR), BF16), ((LATE + 1, HEADS, PAIR, BLK), BF16),
        ((width, width), BF16), ((width, width), BF16),
    ]
    middle = pl.pallas_call(
        functools.partial(kernel, blocks),
        out_shape=[jax.ShapeDtypeStruct(*shape) for shape in shapes],
        in_specs=[hbm, vmem, hbm, hbm, smem, smem, smem],
        out_specs=[hbm] * len(shapes),
        scratch_shapes=[
            pltpu.VMEM((rows, width), F32),
            pltpu.VMEM((rows, width), F32),
            pltpu.VMEM((rows, width), F32),
            pltpu.VMEM((2 * BLK, width), F32),
            pltpu.VMEM((8, BLK), F32),
            pltpu.VMEM((4, 8, BLK), F32),
            pltpu.VMEM((4, width, width), BF16),
            pltpu.VMEM((4, width, width), BF16),
            pltpu.VMEM((groups, width, 2 * BLK), BF16),
            pltpu.VMEM((groups, width, 2 * BLK), BF16),
            pltpu.VMEM((blocks + 1, HEADS, BLK, 2 * PAIR), BF16),
            pltpu.VMEM((blocks + 1, HEADS, PAIR, BLK), BF16),
            pltpu.VMEM((blocks + 1, HEADS, BLK, 2 * PAIR), BF16),
            pltpu.VMEM((blocks + 1, HEADS, PAIR, BLK), BF16),
            pltpu.VMEM((groups, width, 2 * BLK), F32),
            pltpu.VMEM((groups, HEADS, 8, 2 * BLK), F32),
            pltpu.VMEM((groups, HEADS, 8, 2 * BLK), F32),
            dma((chunks,)), dma((chunks,)), dma((chunks,)), dma((chunks,)),
            dma((2,)), dma((2,)), dma((4,)), dma((4,)),
            dma((groups,)), dma((8,)), dma((3, groups)), dma((2, groups)), dma((3, 2)), dma((2,)),
        ],
        compiler_params=pltpu.CompilerParams(
            collective_id=0, has_side_effects=True, vmem_limit_bytes=60 * 1024 * 1024
        ),
    )(points, norm_gain.reshape(1, width), w_qkv, w_out, counts, partner, cross_list[0].T)

    mixed = pl.pallas_call(
        functools.partial(finish_kernel, blocks),
        out_shape=jax.ShapeDtypeStruct((rows, width), F32),
        in_specs=[smem, smem] + [hbm] * (len(shapes) + 1),
        out_specs=hbm,
        scratch_shapes=[pltpu.VMEM(*shape) for shape in shapes]
        + [pltpu.VMEM((rows, width), F32), dma((4, groups)), dma((7,)), dma((groups,))],
        compiler_params=pltpu.CompilerParams(vmem_limit_bytes=60 * 1024 * 1024),
    )(counts, cross_list[0].T, *middle, points)
    return mixed[None]


def solution(mesh):
    in_specs = (
        P("line", "seg", None),
        P(),
        P(),
        P(),
        P("line", "seg"),
        P("line", "seg"),
        P("line", "seg", None),
    )
    out_specs = P("line", "seg", None)
    return jax.shard_map(body, mesh=mesh, in_specs=in_specs, out_specs=out_specs, check_vma=False)
```
